128 devices in a mesh: tm: 4 (over y_hi, core), seq: 32 (over y_lo, x, z).
Axes of the slice: x: 4, y: 4 (y_hi: 2, y_lo: 2; y = y_hi * 2 + y_lo), z: 4, core: 2. Of those that a mesh axis runs over, the one named last changes fastest.
Arguments:
- queries: bfloat16 [65536, 3072], P(('tm', 'seq')), as said below
- keys: bfloat16 [65536, 3072], P(('tm', 'seq')), may hold values from -6 to 6
- values: bfloat16 [65536, 3072], P(('tm', 'seq')), may hold values from -6 to 6
- stale_keys: bfloat16 [65536, 3072], P(('tm', 'seq')), may hold values from -6 to 6
- stale_values: bfloat16 [65536, 3072], P(('tm', 'seq')), may hold values from -6 to 6
- tile_mask: int32 [512, 7, 4], P(('tm', 'seq')), may hold values 0 or 1
- stale_pick: int32 [128, 4], P(('tm', 'seq')), may hold values from 0 to 3
Outputs:
- attended: bfloat16 [65536, 3072], P(('tm', 'seq'))
The draws below stay inside these ranges and needn't reach their ends.
Inputs may be any that keep to these rules, and one draw needn't show every extreme that they name: Rows of the queries have varying scales.
All inputs are finite; a program needn't handle non-finite values. No bound on the sum of `tile_mask` on one device may be relied on, other than what follows from the above.
Results may differ from the reference program's by a relative error of at most 0.0049.
Values may be sent and summed in bfloat16 or wider, within the bound.
A program may use at most 192 MiB of HBM per device.

```python
import jax
import jax.numpy as jnp
from jax import lax

HEADS = 24
HEAD_DIM = 128
MODEL_WIDTH = 3072
TILE_TOKENS = 128
SIDE_REACH = 3
TILES_DEV = 4
FRESH_WINDOW = 7
DEVICE_TOKENS = 512
TILES = 512
TOKENS = 65536
N_TM = 4
N_SEQ = 32
DEVICES = 128


def draw_queries(key, part):
    base = jax.random.normal(jax.random.fold_in(key, 11), (TOKENS, MODEL_WIDTH), jnp.float32)
    base = jnp.clip(base, -6.0, 6.0)
    spread = jax.random.uniform(jax.random.fold_in(key, 13), (TOKENS, 1), jnp.float32, 0.0, 1.0)
    rows = jnp.exp(spread * jnp.log(3.0))
    return (base * rows).astype(jnp.bfloat16)


def touch_ends(drawn, stream_key, smallest, high):
    extent = drawn.shape
    index_at = [jax.random.randint(jax.random.fold_in(stream_key, axis), (), 0, extent[axis]) for axis in range(len(extent))]
    drawn = drawn.at[tuple(index_at)].set(smallest)
    longest = extent.index(max(extent))
    index_at[longest] = (index_at[longest] + 1) % extent[longest]
    return drawn.at[tuple(index_at)].set(high)


def block_scale(key, dims, cuts, smallest, high):
    gain, own = 1.0, jax.random.fold_in(key, 6)
    for dim, blocks in cuts:
        draws = jnp.exp(jax.random.uniform(jax.random.fold_in(own, dim), (blocks,), jnp.float32, smallest / len(cuts), high / len(cuts)))
        gain = gain * jnp.repeat(draws, dims[dim] // blocks).reshape([-1 if axis == dim else 1 for axis in range(len(dims))])
    return gain


def bell_draw(own_key, extent, width, most, pieces=(), held_as=jnp.bfloat16):
    level = block_scale(own_key, extent, pieces, -0.22, 0.18) if pieces else 1.0
    drawn = jax.random.normal(own_key, extent, jnp.float32) * width * level
    return jnp.minimum(jnp.maximum(drawn, -most), most).astype(held_as)


def setup_inputs(seed: int = 0) -> dict:
    splits = jax.random.split(jax.random.key(seed), 8)
    queries = draw_queries(jax.random.fold_in(splits[7], 71), 0)
    keys = bell_draw(splits[1], (TOKENS, MODEL_WIDTH), 1.0, 6.0, ((0, 128),))
    values = bell_draw(splits[2], (TOKENS, MODEL_WIDTH), 1.0, 6.0, ((0, 128),))
    stale_keys = bell_draw(splits[3], (TOKENS, MODEL_WIDTH), 1.0, 6.0, ((0, 128),))
    stale_values = bell_draw(splits[4], (TOKENS, MODEL_WIDTH), 1.0, 6.0, ((0, 128),))
    tile_mask = touch_ends((jax.random.randint(splits[5], (TILES, FRESH_WINDOW, TILES_DEV), 0, 2) < 1).astype(jnp.int32), jax.random.fold_in(splits[5], 1), 0, 1)
    stale_pick = touch_ends(jax.random.randint(splits[6], (DEVICES, N_TM), 0, TILES_DEV), jax.random.fold_in(splits[6], 1), 0, TILES_DEV - 1).astype(jnp.int32)
    return dict(queries=queries, keys=keys, values=values, stale_keys=stale_keys, stale_values=stale_values, tile_mask=tile_mask, stale_pick=stale_pick)


def attend(qdev, kall, gathered_values, allowed):
    scale = 1.0 / (HEAD_DIM ** 0.5)
    rows = qdev.shape[0]
    count = kall.shape[0]
    qh = qdev.reshape(rows, HEADS, HEAD_DIM).transpose(1, 0, 2)
    kh = kall.reshape(count, HEADS, HEAD_DIM).transpose(1, 0, 2)
    vh = gathered_values.reshape(count, HEADS, HEAD_DIM).transpose(1, 0, 2)

    def one_head(items):
        qa, ka, va = items
        score = jnp.dot(qa, ka.T, preferred_element_type=jnp.float32) * scale
        score = jnp.where(allowed, score, jnp.float32(-1e30))
        top = jnp.max(score, axis=1, keepdims=True)
        expo = jnp.exp(score - top)
        weight = (expo / jnp.sum(expo, axis=1, keepdims=True)).astype(jnp.bfloat16)
        return jnp.dot(weight, va, preferred_element_type=jnp.float32).astype(jnp.bfloat16)

    out = lax.map(one_head, (qh, kh, vh))
    return out.transpose(1, 0, 2).reshape(rows, HEADS * HEAD_DIM)


def allowed_rows(mask_dev, shard_index, nseq):
    offsets = jnp.arange(FRESH_WINDOW, dtype=jnp.int32) - SIDE_REACH
    exists = (shard_index + offsets >= 0) & (shard_index + offsets < nseq)
    tiles = (mask_dev > 0) & exists[None, :, None]
    own = (offsets[None, :, None] == 0) & (jnp.arange(TILES_DEV)[:, None, None] == jnp.arange(TILES_DEV)[None, None, :])
    tiles = (tiles | own).reshape(TILES_DEV, FRESH_WINDOW * TILES_DEV)
    tok = jnp.repeat(jnp.repeat(tiles, TILE_TOKENS, axis=0), TILE_TOKENS, axis=1)
    return jnp.concatenate([tok, jnp.ones((DEVICE_TOKENS, N_TM * TILE_TOKENS), dtype=bool)], axis=1)


def reference(queries, keys, values, stale_keys, stale_values, tile_mask, stale_pick):
    q4 = queries.reshape(N_TM, N_SEQ, DEVICE_TOKENS, MODEL_WIDTH)
    kpad = jnp.pad(keys.reshape(N_TM, N_SEQ, DEVICE_TOKENS, MODEL_WIDTH), ((0, 0), (SIDE_REACH, SIDE_REACH), (0, 0), (0, 0)))
    padded_values = jnp.pad(values.reshape(N_TM, N_SEQ, DEVICE_TOKENS, MODEL_WIDTH), ((0, 0), (SIDE_REACH, SIDE_REACH), (0, 0), (0, 0)))
    sk = stale_keys.reshape(N_TM, N_SEQ, TILES_DEV, TILE_TOKENS, MODEL_WIDTH)
    sv = stale_values.reshape(N_TM, N_SEQ, TILES_DEV, TILE_TOKENS, MODEL_WIDTH)
    masks = tile_mask.reshape(N_TM, N_SEQ, TILES_DEV, FRESH_WINDOW, TILES_DEV)
    picks = stale_pick.reshape(N_TM, N_SEQ, N_TM)
    tile_groups = jnp.arange(N_TM, dtype=jnp.int32)

    def device(index):
        group_index = (index // N_SEQ).astype(jnp.int32)
        shard_index = (index % N_SEQ).astype(jnp.int32)
        qdev = q4[group_index, shard_index]
        kwin = lax.dynamic_slice_in_dim(kpad[group_index], shard_index, FRESH_WINDOW, 0).reshape(FRESH_WINDOW * DEVICE_TOKENS, MODEL_WIDTH)
        window_values = lax.dynamic_slice_in_dim(padded_values[group_index], shard_index, FRESH_WINDOW, 0).reshape(FRESH_WINDOW * DEVICE_TOKENS, MODEL_WIDTH)
        chosen_tiles = lax.dynamic_index_in_dim(picks, shard_index, 1, keepdims=False)[:, group_index]
        kcol = lax.dynamic_index_in_dim(sk, shard_index, 1, keepdims=False)
        value_column = lax.dynamic_index_in_dim(sv, shard_index, 1, keepdims=False)
        kst = kcol[tile_groups, chosen_tiles].reshape(N_TM * TILE_TOKENS, MODEL_WIDTH)
        stale_value_rows = value_column[tile_groups, chosen_tiles].reshape(N_TM * TILE_TOKENS, MODEL_WIDTH)
        allowed = allowed_rows(masks[group_index, shard_index], shard_index, N_SEQ)
        kall = jnp.concatenate([kwin, kst], axis=0)
        gathered_values = jnp.concatenate([window_values, stale_value_rows], axis=0)
        return attend(qdev, kall, gathered_values, allowed)

    out = lax.map(device, jnp.arange(N_TM * N_SEQ, dtype=jnp.int32))
    return out.reshape(TOKENS, MODEL_WIDTH)
```

```python
import functools
import math

import jax
import jax.numpy as jnp
from jax import lax
from jax.experimental import pallas as pl
from jax.experimental.pallas import tpu as pltpu
from jax.sharding import PartitionSpec as P

HEADS = 24
HEAD_DIM = 128
TILE = 128
TILES_DEV = 4
REACH = 3
WINDOW = 2 * REACH + 1
ROWS = TILE * TILES_DEV
WIDTH = HEADS * HEAD_DIM
GROUPS = 4
SHARDS = 32
RING = 4
OWN_HEADS = HEADS // RING
SLOTS = RING + 2 * REACH
KEYS = WINDOW * ROWS
STALE = GROUPS * TILE
BLOCK = 256
FACTOR = math.log2(math.e) / math.sqrt(HEAD_DIM)
LOW = -1e30
MESH = pl.DeviceIdType.MESH
BF16 = jnp.bfloat16
F32 = jnp.float32


def scores(q, k):
    return lax.dot_general(q, k, (((1,), (1,)), ((), ())), preferred_element_type=F32) * FACTOR


def kernel(
    q_hbm, k_hbm, v_hbm, sk_hbm, sv_hbm, mask_ref, pick_ref, out_ref,
    kv, qr, ob, oh, stale, stale_out, staging, qh, allow, sc, lse_out, lse_in,
    kv_ss, kv_rs, q_ss, q_rs, halo_ss, halo_rs, o_ss, o_rs, l_ss, l_rs,
    a_ss, a_rs, st_ss, st_rs, loc,
):
    tm = lax.axis_index("tm")
    s = lax.axis_index("seq")
    z = lax.rem(s, RING)
    row0 = s - z
    has_low = s >= RING
    has_high = s < SHARDS - RING

    def ring(d):
        return (tm, row0 + lax.rem(z + d, RING))

    def group(d):
        return (lax.rem(tm + d, GROUPS), s)

    bar = pltpu.get_barrier_semaphore()
    for d in range(1, RING):
        pl.semaphore_signal(bar, inc=1, device_id=ring(d), device_id_type=MESH)
    for d in range(1, GROUPS):
        pl.semaphore_signal(bar, inc=1, device_id=group(d), device_id_type=MESH)

    @pl.when(has_low)
    def _():
        pl.semaphore_signal(bar, inc=1, device_id=(tm, s - RING), device_id_type=MESH)

    @pl.when(has_high)
    def _():
        pl.semaphore_signal(bar, inc=1, device_id=(tm, s + RING), device_id_type=MESH)

    pltpu.make_async_copy(q_hbm, qh, loc.at[0]).start()
    pltpu.make_async_copy(sk_hbm, staging.at[0], loc.at[1]).start()
    pltpu.make_async_copy(sv_hbm, staging.at[1], loc.at[2]).start()

    for t in range(TILES_DEV):
        for o in range(WINDOW):
            there = ((s + (o - REACH) >= 0) & (s + (o - REACH) < SHARDS)).astype(F32)
            for j in range(TILES_DEV):
                if o == REACH and j == t:
                    value = jnp.ones((1, TILE), F32)
                else:
                    value = jnp.full((1, TILE), mask_ref[t, o, j], jnp.int32).astype(F32) * there
                allow[z, pl.ds(t * 32 + o * TILES_DEV + j, 1), :] = value

    pl.semaphore_wait(
        bar, RING - 1 + GROUPS - 1 + has_low.astype(jnp.int32) + has_high.astype(jnp.int32)
    )

    def kv_copy(i, d, which):
        src = (k_hbm, v_hbm)[which]
        head = lax.rem(z + d, RING) * OWN_HEADS + i
        cols = pl.ds(pl.multiple_of(head * HEAD_DIM, HEAD_DIM), HEAD_DIM)
        rows = pl.ds(pl.multiple_of((REACH + z) * ROWS, ROWS), ROWS)
        dst = kv.at[i, which, rows, :]
        if d == 0:
            return pltpu.make_async_copy(src.at[:, cols], dst, kv_rs.at[i, d, which])
        return pltpu.make_async_remote_copy(
            src.at[:, cols], dst, kv_ss.at[i, d, which], kv_rs.at[i, d, which],
            device_id=ring(d), device_id_type=MESH)

    def q_copy(i, d):
        head = lax.rem(z + d, RING) * OWN_HEADS + i
        cols = pl.ds(pl.multiple_of(head * HEAD_DIM, HEAD_DIM), HEAD_DIM)
        dst = qr.at[i, pl.ds(pl.multiple_of(z * ROWS, ROWS), ROWS), :]
        if d == 0:
            return pltpu.make_async_copy(q_hbm.at[:, cols], dst, q_rs.at[i, d])
        return pltpu.make_async_remote_copy(
            q_hbm.at[:, cols], dst, q_ss.at[i, d], q_rs.at[i, d],
            device_id=ring(d), device_id_type=MESH)

    def allow_copy(d):
        return pltpu.make_async_remote_copy(
            allow.at[z], allow.at[z], a_ss.at[d], a_rs.at[d],
            device_id=ring(d), device_id_type=MESH)

    def halo_copy(i, up):
        if up:
            src = kv.at[i, :, pl.ds((RING) * ROWS, REACH * ROWS), :]
            dst = kv.at[i, :, pl.ds(0, REACH * ROWS), :]
            dev = (tm, s + RING)
        else:
            src = kv.at[i, :, pl.ds(REACH * ROWS, REACH * ROWS), :]
            dst = kv.at[i, :, pl.ds((RING + REACH) * ROWS, REACH * ROWS), :]
            dev = (tm, s - RING)
        n = 0 if up else 1
        return pltpu.make_async_remote_copy(
            src, dst, halo_ss.at[i, n], halo_rs.at[i, n], device_id=dev, device_id_type=MESH)

    def o_copy(i, d):
        j = lax.rem(z + d, RING)
        return pltpu.make_async_remote_copy(
            ob.at[i, pl.ds(pl.multiple_of(j * ROWS, ROWS), ROWS), :], oh.at[i, z],
            o_ss.at[i, d], o_rs.at[i, d], device_id=ring(d), device_id_type=MESH)

    def l_copy(i, d):
        j = lax.rem(z + d, RING)
        return pltpu.make_async_remote_copy(
            lse_out.at[i, j], lse_in.at[i, z],
            l_ss.at[i, d], l_rs.at[i, d], device_id=ring(d), device_id_type=MESH)

    def stale_copy(d):
        return pltpu.make_async_remote_copy(
            stale_out.at[d - 1], stale.at[:, pl.ds(pl.multiple_of(tm * TILE, TILE), TILE), :],
            st_ss.at[d], st_rs.at[d], device_id=group(d), device_id_type=MESH)

    def start_kv(i):
        for d in (2, 1, 3, 0):
            for which in range(2):
                kv_copy(i, d, which).start()

    def start_q(i):
        for d in (2, 1, 3, 0):
            q_copy(i, d).start()

    def halo(i):
        for d in range(RING):
            for which in range(2):
                if d == 0:
                    kv_copy(i, d, which).wait()
                else:
                    kv_copy(i, d, which).wait_recv()

        @pl.when(has_high)
        def _():
            halo_copy(i, True).start()

        @pl.when(has_low)
        def _():
            halo_copy(i, False).start()

    for d in range(1, RING):
        allow_copy(d).start()
    start_kv(0)
    start_kv(1)
    start_q(0)

    @pl.when(jnp.logical_not(has_low))
    def _():
        @pl.loop(0, OWN_HEADS)
        def _(i):
            for which in range(2):
                kv[i, which, pl.ds(0, REACH * ROWS), :] = jnp.zeros((REACH * ROWS, HEAD_DIM), BF16)

    @pl.when(jnp.logical_not(has_high))
    def _():
        @pl.loop(0, OWN_HEADS)
        def _(i):
            for which in range(2):
                kv[i, which, pl.ds((RING + REACH) * ROWS, REACH * ROWS), :] = jnp.zeros(
                    (REACH * ROWS, HEAD_DIM), BF16)

    pltpu.make_async_copy(sk_hbm, staging.at[0], loc.at[1]).wait()
    pltpu.make_async_copy(sv_hbm, staging.at[1], loc.at[2]).wait()
    for d in (2, 1, 3, 0):
        tile = pick_ref[0, lax.rem(tm + d, GROUPS)]
        chosen = [
            (1 - jnp.minimum(jnp.abs(jnp.full((TILE, TILE), tile, jnp.int32) - t), 1)).astype(F32).astype(BF16)
            for t in range(TILES_DEV)
        ]
        for which in range(2):
            @pl.loop(0, HEADS)
            def _(h, d=d, which=which, chosen=chosen):
                cols = pl.ds(pl.multiple_of(h * HEAD_DIM, HEAD_DIM), HEAD_DIM)
                one = [staging[which, pl.ds(t * TILE, TILE), cols] * chosen[t] for t in range(TILES_DEV)]
                one = (one[0] + one[1]) + (one[2] + one[3])
                if d == 0:
                    stale[which, pl.ds(pl.multiple_of(tm * TILE, TILE), TILE), cols] = one
                else:
                    stale_out[d - 1, which, :, cols] = one
        if d:
            stale_copy(d).start()

    halo(0)
    for d in range(1, RING):
        allow_copy(d).wait_recv()
    pltpu.make_async_copy(q_hbm, qh, loc.at[0]).wait()

    def fresh(i):
        @pl.loop(0, RING * ROWS // BLOCK)
        def _(n):
            j = n // (ROWS // BLOCK)
            b = n % (ROWS // BLOCK)
            q = qr[i, pl.ds(pl.multiple_of(n * BLOCK, BLOCK), BLOCK), :]
            base = j * ROWS
            mx = None
            for c in range(WINDOW):
                k = kv[i, 0, pl.ds(pl.multiple_of(base + c * ROWS, ROWS), ROWS), :]
                x = scores(q, k)
                parts = []
                for tt in range(BLOCK // TILE):
                    t = b * (BLOCK // TILE) + tt
                    row = []
                    for kk in range(TILES_DEV):
                        a = allow[j, pl.ds(t * 32 + c * TILES_DEV + kk, 1), :]
                        y = x[tt * TILE:(tt + 1) * TILE, kk * TILE:(kk + 1) * TILE]
                        y = jnp.where(a > 0, y, LOW)
                        sc[tt * TILE:(tt + 1) * TILE, pl.ds(c * ROWS + kk * TILE, TILE)] = y
                        row.append(y)
                    parts.append(jnp.maximum(jnp.maximum(row[0], row[1]), jnp.maximum(row[2], row[3])))
                x = jnp.concatenate(parts, axis=0)
                mx = x if mx is None else jnp.maximum(mx, x)
            m = jnp.max(mx, axis=1, keepdims=True)
            total = jnp.zeros((BLOCK, TILE), F32)
            acc = jnp.zeros((BLOCK, HEAD_DIM), F32)
            for c in range(WINDOW):
                p = jnp.exp2(sc[:, pl.ds(c * ROWS, ROWS)] - m)
                for kk in range(TILES_DEV):
                    total += p[:, kk * TILE:(kk + 1) * TILE]
                v = kv[i, 1, pl.ds(pl.multiple_of(base + c * ROWS, ROWS), ROWS), :]
                acc += jnp.dot(p.astype(BF16), v, preferred_element_type=F32)
            total = jnp.sum(total, axis=1, keepdims=True)
            o = (acc / total).astype(BF16)
            ob[i, pl.ds(pl.multiple_of(n * BLOCK, BLOCK), BLOCK), :] = o
            lse = jnp.broadcast_to(m + jnp.log2(total), (BLOCK, TILE))
            for tt in range(BLOCK // TILE):
                turned = lse[tt * TILE:(tt + 1) * TILE, :].T
                lse_out[i, j, pl.ds(b * (BLOCK // TILE) + tt, 1), :] = turned[0:1, :]

    def send_home(i):
        for d in range(1, RING):
            o_copy(i, d).start()
            l_copy(i, d).start()
        oh[i, z] = ob[i, pl.ds(pl.multiple_of(z * ROWS, ROWS), ROWS), :]
        lse_in[i, z] = lse_out[i, z]

    def merge(i):
        for d in range(1, RING):
            o_copy(i, d).wait_recv()
            l_copy(i, d).wait_recv()

        @pl.loop(0, RING * ROWS // BLOCK)
        def _(n):
            owner = n // (ROWS // BLOCK)
            b = n % (ROWS // BLOCK)
            head = owner * OWN_HEADS + i
            cols = pl.ds(pl.multiple_of(head * HEAD_DIM, HEAD_DIM), HEAD_DIM)
            rows = pl.ds(pl.multiple_of(b * BLOCK, BLOCK), BLOCK)
            x = scores(qh[rows, cols], stale[0, :, cols])
            lse = []
            for tt in range(BLOCK // TILE):
                one = lse_in[i, owner, pl.ds(b * (BLOCK // TILE) + tt, 1), :]
                lse.append(jnp.broadcast_to(one, (TILE, TILE)).T)
            lse = jnp.concatenate(lse, axis=0)
            m = jnp.maximum(jnp.max(x, axis=1, keepdims=True), lse)
            old = jnp.exp2(lse - m)
            p = [jnp.exp2(x[:, k * TILE:(k + 1) * TILE] - m) for k in range(GROUPS)]
            total = old + jnp.sum(p[0] + p[1] + p[2] + p[3], axis=1, keepdims=True)
            acc = jnp.dot(jnp.concatenate(p, axis=1).astype(BF16), stale[1, :, cols],
                          preferred_element_type=F32)
            o = oh[i, owner, rows, :].astype(F32)
            out_ref[rows, cols] = ((old * o + acc) / total).astype(BF16)

    @pl.loop(0, OWN_HEADS)
    def _(i):
        @pl.when(i < OWN_HEADS - 2)
        def _():
            start_kv(i + 2)

        @pl.when(i < OWN_HEADS - 1)
        def _():
            start_q(i + 1)
            halo(i + 1)

        @pl.when(i == 2)
        def _():
            for d in range(1, GROUPS):
                stale_copy(d).wait_recv()

        @pl.when(i >= 2)
        def _():
            merge(i - 2)

        for d in range(RING):
            if d == 0:
                q_copy(i, d).wait()
            else:
                q_copy(i, d).wait_recv()

        @pl.when(has_low)
        def _():
            halo_copy(i, True).wait_recv()

        @pl.when(has_high)
        def _():
            halo_copy(i, False).wait_recv()

        fresh(i)
        send_home(i)

    @pl.loop(OWN_HEADS - 2, OWN_HEADS)
    def _(i):
        merge(i)

    for d in range(1, RING):
        allow_copy(d).wait_send()
    for d in range(1, GROUPS):
        stale_copy(d).wait_send()

    @pl.loop(0, OWN_HEADS)
    def _(i):
        for d in range(1, RING):
            for which in range(2):
                kv_copy(i, d, which).wait_send()
            q_copy(i, d).wait_send()
            o_copy(i, d).wait_send()
            l_copy(i, d).wait_send()

        @pl.when(has_high)
        def _():
            halo_copy(i, True).wait_send()

        @pl.when(has_low)
        def _():
            halo_copy(i, False).wait_send()


def body(queries, keys, values, stale_keys, stale_values, tile_mask, stale_pick):
    dma = pltpu.SemaphoreType.DMA
    hbm = pl.BlockSpec(memory_space=pl.ANY)
    smem = pl.BlockSpec(memory_space=pltpu.SMEM)
    return pl.pallas_call(
        kernel,
        out_shape=jax.ShapeDtypeStruct((ROWS, WIDTH), BF16),
        in_specs=[hbm] * 5 + [smem] * 2,
        out_specs=pl.BlockSpec(memory_space=pltpu.VMEM),
        scratch_shapes=[
            pltpu.VMEM((OWN_HEADS, 2, SLOTS * ROWS, HEAD_DIM), BF16),
            pltpu.VMEM((OWN_HEADS, RING * ROWS, HEAD_DIM), BF16),
            pltpu.VMEM((OWN_HEADS, RING * ROWS, HEAD_DIM), BF16),
            pltpu.VMEM((OWN_HEADS, RING, ROWS, HEAD_DIM), BF16),
            pltpu.VMEM((2, STALE, WIDTH), BF16),
            pltpu.VMEM((GROUPS - 1, 2, TILE, WIDTH), BF16),
            pltpu.VMEM((2, ROWS, WIDTH), BF16),
            pltpu.VMEM((ROWS, WIDTH), BF16),
            pltpu.VMEM((RING, TILE, TILE), F32),
            pltpu.VMEM((BLOCK, KEYS), F32),
            pltpu.VMEM((OWN_HEADS, RING, 8, TILE), F32),
            pltpu.VMEM((OWN_HEADS, RING, 8, TILE), F32),
            dma((OWN_HEADS, RING, 2)), dma((OWN_HEADS, RING, 2)),
            dma((OWN_HEADS, RING)), dma((OWN_HEADS, RING)),
            dma((OWN_HEADS, 2)), dma((OWN_HEADS, 2)),
            dma((OWN_HEADS, RING)), dma((OWN_HEADS, RING)),
            dma((OWN_HEADS, RING)), dma((OWN_HEADS, RING)),
            dma((RING,)), dma((RING,)),
            dma((GROUPS,)), dma((GROUPS,)),
            dma((3,)),
        ],
        compiler_params=pltpu.CompilerParams(
            collective_id=0, has_side_effects=True, vmem_limit_bytes=58 * 2**20
        ),
        cost_estimate=pl.CostEstimate(
            flops=4 * ROWS * HEAD_DIM * HEADS * (KEYS + STALE),
            bytes_accessed=8 * ROWS * WIDTH * 2,
            transcendentals=ROWS * HEADS * (KEYS + STALE),
        ),
    )(queries, keys, values, stale_keys, stale_values, tile_mask, stale_pick)


def solution(mesh):
    wide = P(("tm", "seq"), None)
    placed = (wide, wide, wide, wide, wide, P(("tm", "seq"), None, None), wide)
    return jax.shard_map(body, mesh=mesh, in_specs=placed, out_specs=wide, check_vma=False)
```

```python
import functools
import math

import jax
import jax.numpy as jnp
from jax import lax
from jax.experimental import pallas as pl
from jax.experimental.pallas import tpu as pltpu
from jax.sharding import PartitionSpec as P

HEADS = 24
HEAD_DIM = 128
TILE = 128
TILES_DEV = 4
REACH = 3
WINDOW = 2 * REACH + 1
ROWS = TILE * TILES_DEV
WIDTH = HEADS * HEAD_DIM
GROUPS = 4
SHARDS = 32
RUNS = 8
LATE = 4
MIDDLE = RUNS // 2
RING = 4
OWN_HEADS = HEADS // RING
SLOTS = RING + 2 * REACH
KEYS = WINDOW * ROWS
STALE = GROUPS * TILE
BLOCK = 256
HALF = REACH * ROWS // 2
FACTOR = math.log2(math.e) / math.sqrt(HEAD_DIM)
LOW = -1e30
MESH = pl.DeviceIdType.MESH
BF16 = jnp.bfloat16
F32 = jnp.float32


def scores(q, k):
    return lax.dot_general(q, k, (((1,), (1,)), ((), ())), preferred_element_type=F32)


def with_sums(p, v):
    ones = jnp.ones((v.shape[0], HEAD_DIM), BF16)
    return jnp.dot(p, jnp.concatenate([v, ones], axis=1), preferred_element_type=F32)


def kernel(
    q_hbm, k_hbm, v_hbm, sk_hbm, sv_hbm, mask_ref, pick_ref, out_ref,
    kv, qr, ob, oh, stale, stale_out, staging, qh, allow, sc_a, sc_b, top_a, top_b, lse_out, lse_in,
    kv_ss, kv_rs, q_ss, q_rs, halo_ss, halo_rs, relay_rs, pass_ss, o_ss, o_rs, l_ss, l_rs,
    a_ss, a_rs, st_ss, st_rs, loc,
):
    tm = lax.axis_index("tm")
    s = lax.axis_index("seq")
    z = lax.rem(s, RING)
    row0 = s - z
    run = s // RING
    has_low = s >= RING
    has_high = s < SHARDS - RING
    mid_low = run == MIDDLE - 1
    mid_high = run == MIDDLE
    first_run = run == 0
    last_run = run == RUNS - 1
    corner = first_run | mid_low | mid_high | last_run
    near = jnp.where(run < MIDDLE, s + MIDDLE * RING, s - MIDDLE * RING)
    far = jnp.where(first_run | mid_high, s + (MIDDLE - 1) * RING, s - (MIDDLE - 1) * RING)

    def ring(d):
        return (tm, row0 + lax.rem(z + d, RING))

    def group(d):
        return (lax.rem(tm + d, GROUPS), s)

    bar = pltpu.get_barrier_semaphore()
    for d in range(1, RING):
        pl.semaphore_signal(bar, inc=1, device_id=ring(d), device_id_type=MESH)
    for d in range(1, GROUPS):
        pl.semaphore_signal(bar, inc=1, device_id=group(d), device_id_type=MESH)

    @pl.when(has_low)
    def _():
        pl.semaphore_signal(bar, inc=1, device_id=(tm, s - RING), device_id_type=MESH)

    @pl.when(has_high)
    def _():
        pl.semaphore_signal(bar, inc=1, device_id=(tm, s + RING), device_id_type=MESH)

    @pl.when(corner)
    def _():
        pl.semaphore_signal(bar, inc=1, device_id=(tm, near), device_id_type=MESH)
        pl.semaphore_signal(bar, inc=1, device_id=(tm, far), device_id_type=MESH)

    pltpu.make_async_copy(q_hbm, qh, loc.at[0]).start()
    pltpu.make_async_copy(sk_hbm, staging.at[0], loc.at[1]).start()
    pltpu.make_async_copy(sv_hbm, staging.at[1], loc.at[2]).start()

    for t in range(TILES_DEV):
        for o in range(WINDOW):
            there = ((s + (o - REACH) >= 0) & (s + (o - REACH) < SHARDS)).astype(F32)
            for j in range(TILES_DEV):
                if o == REACH and j == t:
                    value = jnp.ones((1, TILE), F32)
                else:
                    value = jnp.full((1, TILE), mask_ref[t, o, j], jnp.int32).astype(F32) * there
                allow[z, pl.ds(t * 32 + o * TILES_DEV + j, 1), :] = value

    pl.semaphore_wait(
        bar,
        RING - 1 + GROUPS - 1 + has_low.astype(jnp.int32) + has_high.astype(jnp.int32)
        + 2 * corner.astype(jnp.int32),
    )

    def kv_copy(i, d, which):
        src = (k_hbm, v_hbm)[which]
        head = lax.rem(z + d, RING) * OWN_HEADS + i
        cols = pl.ds(pl.multiple_of(head * HEAD_DIM, HEAD_DIM), HEAD_DIM)
        rows = pl.ds(pl.multiple_of((REACH + z) * ROWS, ROWS), ROWS)
        dst = kv.at[i, which, rows, :]
        if d == 0:
            return pltpu.make_async_copy(src.at[:, cols], dst, kv_rs.at[i, d, which])
        return pltpu.make_async_remote_copy(
            src.at[:, cols], dst, kv_ss.at[i, d, which], kv_rs.at[i, d, which],
            device_id=ring(d), device_id_type=MESH)

    def q_copy(i, d):
        head = lax.rem(z + d, RING) * OWN_HEADS + i
        cols = pl.ds(pl.multiple_of(head * HEAD_DIM, HEAD_DIM), HEAD_DIM)
        dst = qr.at[i, pl.ds(pl.multiple_of(z * ROWS, ROWS), ROWS), :]
        if d == 0:
            return pltpu.make_async_copy(q_hbm.at[:, cols], dst, q_rs.at[i, d])
        return pltpu.make_async_remote_copy(
            q_hbm.at[:, cols], dst, q_ss.at[i, d], q_rs.at[i, d],
            device_id=ring(d), device_id_type=MESH)

    def allow_copy(d):
        return pltpu.make_async_remote_copy(
            allow.at[z], allow.at[z], a_ss.at[d], a_rs.at[d],
            device_id=ring(d), device_id_type=MESH)

    LOW_SLOTS, OWN_LOW, OWN_HIGH, HIGH_SLOTS = 0, REACH * ROWS, RING * ROWS, (RING + REACH) * ROWS

    def halo_copy(i, up, half):
        start, land = (OWN_HIGH, LOW_SLOTS) if up else (OWN_LOW, HIGH_SLOTS)
        n = 0 if up else 1
        return pltpu.make_async_remote_copy(
            kv.at[i, :, pl.ds(start + half * HALF, HALF), :],
            kv.at[i, :, pl.ds(land + half * HALF, HALF), :],
            halo_ss.at[i, n, half], halo_rs.at[i, n, half],
            device_id=(tm, s + RING if up else s - RING), device_id_type=MESH)

    def relay_copy(i, up):
        start, land = (OWN_HIGH, HIGH_SLOTS) if up else (OWN_LOW, LOW_SLOTS)
        n = 0 if up else 1
        return pltpu.make_async_remote_copy(
            kv.at[i, :, pl.ds(start + HALF, HALF), :], kv.at[i, :, pl.ds(land, HALF), :],
            halo_ss.at[i, n, 1], relay_rs.at[i], device_id=(tm, near), device_id_type=MESH)

    def pass_copy(i, up):
        start, land = (HIGH_SLOTS, LOW_SLOTS) if up else (LOW_SLOTS, HIGH_SLOTS)
        n = 0 if up else 1
        return pltpu.make_async_remote_copy(
            kv.at[i, :, pl.ds(start, HALF), :], kv.at[i, :, pl.ds(land + HALF, HALF), :],
            pass_ss.at[i], halo_rs.at[i, n, 1], device_id=(tm, far), device_id_type=MESH)

    def hand_on(i):
        @pl.when(last_run)
        def _():
            relay_copy(i, True).wait_recv()
            pass_copy(i, True).start()

        @pl.when(first_run)
        def _():
            relay_copy(i, False).wait_recv()
            pass_copy(i, False).start()

    def o_copy(i, d):
        j = lax.rem(z + d, RING)
        return pltpu.make_async_remote_copy(
            ob.at[i, pl.ds(pl.multiple_of(j * ROWS, ROWS), ROWS), :], oh.at[i, z],
            o_ss.at[i, d], o_rs.at[i, d], device_id=ring(d), device_id_type=MESH)

    def l_copy(i, d):
        j = lax.rem(z + d, RING)
        return pltpu.make_async_remote_copy(
            lse_out.at[i, j], lse_in.at[i, z],
            l_ss.at[i, d], l_rs.at[i, d], device_id=ring(d), device_id_type=MESH)

    def stale_copy(d):
        return pltpu.make_async_remote_copy(
            stale_out.at[d - 1], stale.at[:, pl.ds(pl.multiple_of(tm * TILE, TILE), TILE), :],
            st_ss.at[d], st_rs.at[d], device_id=group(d), device_id_type=MESH)

    def start_kv(i):
        for d in (2, 1, 3, 0):
            for which in range(2):
                kv_copy(i, d, which).start()

    def start_q(i):
        for d in (2, 1, 3, 0):
            q_copy(i, d).start()

    def halo(i):
        for d in range(RING):
            for which in range(2):
                if d == 0:
                    kv_copy(i, d, which).wait()
                else:
                    kv_copy(i, d, which).wait_recv()

        @pl.when(has_high)
        def _():
            halo_copy(i, True, 0).start()

        @pl.when(has_low)
        def _():
            halo_copy(i, False, 0).start()

        @pl.when(has_high & jnp.logical_not(mid_low))
        def _():
            halo_copy(i, True, 1).start()

        @pl.when(has_low & jnp.logical_not(mid_high))
        def _():
            halo_copy(i, False, 1).start()

        @pl.when(mid_low)
        def _():
            relay_copy(i, True).start()

        @pl.when(mid_high)
        def _():
            relay_copy(i, False).start()

    for d in range(1, RING):
        allow_copy(d).start()
    @pl.loop(0, OWN_HEADS)
    def _(i):
        start_kv(i)
        start_q(i)

    @pl.when(jnp.logical_not(has_low))
    def _():
        @pl.loop(0, OWN_HEADS)
        def _(i):
            for which in range(2):
                kv[i, which, pl.ds(HALF, HALF), :] = jnp.zeros((HALF, HEAD_DIM), BF16)

    @pl.when(jnp.logical_not(has_high))
    def _():
        @pl.loop(0, OWN_HEADS)
        def _(i):
            for which in range(2):
                kv[i, which, pl.ds((RING + REACH) * ROWS + HALF, HALF), :] = jnp.zeros(
                    (HALF, HEAD_DIM), BF16)

    pltpu.make_async_copy(sk_hbm, staging.at[0], loc.at[1]).wait()
    pltpu.make_async_copy(sv_hbm, staging.at[1], loc.at[2]).wait()
    for d in (2, 1, 3, 0):
        tile = pick_ref[0, lax.rem(tm + d, GROUPS)]
        chosen = [
            (1 - jnp.minimum(jnp.abs(jnp.full((TILE, TILE), tile, jnp.int32) - t), 1)).astype(F32).astype(BF16)
            for t in range(TILES_DEV)
        ]
        for which in range(2):
            @pl.loop(0, HEADS)
            def _(h, d=d, which=which, chosen=chosen):
                cols = pl.ds(pl.multiple_of(h * HEAD_DIM, HEAD_DIM), HEAD_DIM)
                one = [staging[which, pl.ds(t * TILE, TILE), cols] * chosen[t] for t in range(TILES_DEV)]
                one = (one[0] + one[1]) + (one[2] + one[3])
                if d == 0:
                    stale[which, pl.ds(pl.multiple_of(tm * TILE, TILE), TILE), cols] = one
                else:
                    stale_out[d - 1, which, :, cols] = one
        if d:
            stale_copy(d).start()

    halo(0)
    for d in range(1, RING):
        allow_copy(d).wait_recv()
    pltpu.make_async_copy(q_hbm, qh, loc.at[0]).wait()

    PARTS = ROWS // BLOCK

    def both(i, scored, weighed):
        top = acc = None
        if scored is not None:
            h, b, s_ref, top_ref = scored
            j = lax.rem(z + 1 + h, RING)
            q = qr[i, pl.ds(pl.multiple_of(j * ROWS + b * BLOCK, BLOCK), BLOCK), :]
            base = pl.multiple_of(j * ROWS, ROWS)
        if weighed is not None:
            h2, b2, p_ref, ptop_ref = weighed
            j2 = lax.rem(z + 1 + h2, RING)
            base2 = pl.multiple_of(j2 * ROWS, ROWS)
            shift = ptop_ref[...]
            acc = jnp.zeros((BLOCK, 2 * HEAD_DIM), F32)
        for c in range(WINDOW):
            if scored is not None:
                x = scores(q, kv[i, 0, pl.ds(pl.multiple_of(base + c * ROWS, ROWS), ROWS), :])
                parts = []
                for tt in range(BLOCK // TILE):
                    most = None
                    for kk in range(TILES_DEV):
                        pair = (b * (BLOCK // TILE) + tt) * 32 + c * TILES_DEV + kk
                        y = x[tt * TILE:(tt + 1) * TILE, kk * TILE:(kk + 1) * TILE]
                        y = jnp.where(allow[j, pl.ds(pair, 1), :] > 0, y, LOW)
                        s_ref[tt * TILE:(tt + 1) * TILE, pl.ds(c * ROWS + kk * TILE, TILE)] = y
                        most = y if most is None else jnp.maximum(most, y)
                    parts.append(most)
                x = jnp.concatenate(parts, axis=0)
                top = x if top is None else jnp.maximum(top, x)
            if weighed is not None:
                p = [
                    jnp.exp2(p_ref[:, pl.ds(c * ROWS + kk * TILE, TILE)] * FACTOR - shift).astype(BF16)
                    for kk in range(TILES_DEV)
                ]
                v = kv[i, 1, pl.ds(pl.multiple_of(base2 + c * ROWS, ROWS), ROWS), :]
                acc += with_sums(jnp.concatenate(p, axis=1), v)
        if scored is not None:
            top_ref[...] = jnp.broadcast_to(
                jnp.max(top, axis=1, keepdims=True) * FACTOR, (BLOCK, TILE))
        if weighed is not None:
            total = acc[:, HEAD_DIM:]
            ob[i, pl.ds(pl.multiple_of(j2 * ROWS + b2 * BLOCK, BLOCK), BLOCK), :] = (
                acc[:, :HEAD_DIM] / total).astype(BF16)
            lse = shift + jnp.log2(total)
            for tt in range(BLOCK // TILE):
                turned = lse[tt * TILE:(tt + 1) * TILE, :].T
                lse_out[i, j2, pl.ds(b2 * (BLOCK // TILE) + tt, 1), :] = turned[0:1, :]

    def fresh(i):
        a, b = (sc_a, top_a), (sc_b, top_b)
        both(i, (0, 0, *a), None)

        @pl.loop(0, RING - 1)
        def _(h):
            both(i, (h, 1, *b), (h, 0, *a))
            both(i, (h + 1, 0, *a), (h, 1, *b))
            o_copy(i, h + 1).start()
            l_copy(i, h + 1).start()

        both(i, (RING - 1, 1, *b), (RING - 1, 0, *a))
        both(i, None, (RING - 1, 1, *b))
        oh[i, z] = ob[i, pl.ds(pl.multiple_of(z * ROWS, ROWS), ROWS), :]
        lse_in[i, z] = lse_out[i, z]

    def merge(i):
        for d in range(1, RING):
            o_copy(i, d).wait_recv()
            l_copy(i, d).wait_recv()

        @pl.loop(0, RING * ROWS // BLOCK)
        def _(n):
            owner = n // (ROWS // BLOCK)
            b = n % (ROWS // BLOCK)
            head = owner * OWN_HEADS + i
            cols = pl.ds(pl.multiple_of(head * HEAD_DIM, HEAD_DIM), HEAD_DIM)
            rows = pl.ds(pl.multiple_of(b * BLOCK, BLOCK), BLOCK)
            x = scores(qh[rows, cols], stale[0, :, cols]) * FACTOR
            lse = []
            for tt in range(BLOCK // TILE):
                one = lse_in[i, owner, pl.ds(b * (BLOCK // TILE) + tt, 1), :]
                lse.append(jnp.broadcast_to(one, (TILE, TILE)).T)
            lse = jnp.concatenate(lse, axis=0)
            m = jnp.maximum(jnp.max(x, axis=1, keepdims=True), lse)
            old = jnp.exp2(lse - m)
            p = [jnp.exp2(x[:, k * TILE:(k + 1) * TILE] - m) for k in range(GROUPS)]
            acc = with_sums(jnp.concatenate(p, axis=1).astype(BF16), stale[1, :, cols])
            o = oh[i, owner, rows, :].astype(F32)
            out_ref[rows, cols] = (
                (old * o + acc[:, :HEAD_DIM]) / (old + acc[:, HEAD_DIM:])).astype(BF16)

    @pl.loop(0, OWN_HEADS)
    def _(i):
        @pl.when(i < OWN_HEADS - 2)
        def _():
            pass

        @pl.when(i < OWN_HEADS - 1)
        def _():
            halo(i + 1)

        hand_on(i)

        @pl.when(i == LATE)
        def _():
            for d in range(1, GROUPS):
                stale_copy(d).wait_recv()

        @pl.when(i >= LATE)
        def _():
            @pl.loop(2 * (i - LATE), 2 * (i - LATE) + 2)
            def _(n):
                merge(n)

        for d in range(RING):
            if d == 0:
                q_copy(i, d).wait()
            else:
                q_copy(i, d).wait_recv()

        @pl.when(has_low)
        def _():
            halo_copy(i, True, 0).wait_recv()
            halo_copy(i, True, 1).wait_recv()

        @pl.when(has_high)
        def _():
            halo_copy(i, False, 0).wait_recv()
            halo_copy(i, False, 1).wait_recv()

        fresh(i)

    @pl.loop(2 * (OWN_HEADS - LATE), OWN_HEADS)
    def _(i):
        merge(i)

    for d in range(1, RING):
        allow_copy(d).wait_send()
    for d in range(1, GROUPS):
        stale_copy(d).wait_send()

    @pl.loop(0, OWN_HEADS)
    def _(i):
        for d in range(1, RING):
            for which in range(2):
                kv_copy(i, d, which).wait_send()
            q_copy(i, d).wait_send()
            o_copy(i, d).wait_send()
            l_copy(i, d).wait_send()

        @pl.when(has_high)
        def _():
            halo_copy(i, True, 0).wait_send()
            halo_copy(i, True, 1).wait_send()

        @pl.when(has_low)
        def _():
            halo_copy(i, False, 0).wait_send()
            halo_copy(i, False, 1).wait_send()

        @pl.when(last_run | first_run)
        def _():
            pass_copy(i, True).wait_send()


def body(queries, keys, values, stale_keys, stale_values, tile_mask, stale_pick):
    dma = pltpu.SemaphoreType.DMA
    hbm = pl.BlockSpec(memory_space=pl.ANY)
    smem = pl.BlockSpec(memory_space=pltpu.SMEM)
    return pl.pallas_call(
        kernel,
        out_shape=jax.ShapeDtypeStruct((ROWS, WIDTH), BF16),
        in_specs=[hbm] * 5 + [smem] * 2,
        out_specs=pl.BlockSpec(memory_space=pltpu.VMEM),
        scratch_shapes=[
            pltpu.VMEM((OWN_HEADS, 2, SLOTS * ROWS, HEAD_DIM), BF16),
            pltpu.VMEM((OWN_HEADS, RING * ROWS, HEAD_DIM), BF16),
            pltpu.VMEM((OWN_HEADS, RING * ROWS, HEAD_DIM), BF16),
            pltpu.VMEM((OWN_HEADS, RING, ROWS, HEAD_DIM), BF16),
            pltpu.VMEM((2, STALE, WIDTH), BF16),
            pltpu.VMEM((GROUPS - 1, 2, TILE, WIDTH), BF16),
            pltpu.VMEM((2, ROWS, WIDTH), BF16),
            pltpu.VMEM((ROWS, WIDTH), BF16),
            pltpu.VMEM((RING, TILE, TILE), F32),
            pltpu.VMEM((BLOCK, KEYS), F32), pltpu.VMEM((BLOCK, KEYS), F32),
            pltpu.VMEM((BLOCK, TILE), F32), pltpu.VMEM((BLOCK, TILE), F32),
            pltpu.VMEM((OWN_HEADS, RING, 8, TILE), F32),
            pltpu.VMEM((OWN_HEADS, RING, 8, TILE), F32),
            dma((OWN_HEADS, RING, 2)), dma((OWN_HEADS, RING, 2)),
            dma((OWN_HEADS, RING)), dma((OWN_HEADS, RING)),
            dma((OWN_HEADS, 2, 2)), dma((OWN_HEADS, 2, 2)),
            dma((OWN_HEADS,)), dma((OWN_HEADS,)),
            dma((OWN_HEADS, RING)), dma((OWN_HEADS, RING)),
            dma((OWN_HEADS, RING)), dma((OWN_HEADS, RING)),
            dma((RING,)), dma((RING,)),
            dma((GROUPS,)), dma((GROUPS,)),
            dma((3,)),
        ],
        compiler_params=pltpu.CompilerParams(
            collective_id=0, has_side_effects=True, vmem_limit_bytes=58 * 2**20
        ),
        cost_estimate=pl.CostEstimate(
            flops=4 * ROWS * HEAD_DIM * HEADS * (KEYS + STALE),
            bytes_accessed=8 * ROWS * WIDTH * 2,
            transcendentals=ROWS * HEADS * (KEYS + STALE),
        ),
    )(queries, keys, values, stale_keys, stale_values, tile_mask, stale_pick)


def solution(mesh):
    wide = P(("tm", "seq"), None)
    placed = (wide, wide, wide, wide, wide, P(("tm", "seq"), None, None), wide)
    return jax.shard_map(body, mesh=mesh, in_specs=placed, out_specs=wide, check_vma=False)
```

```python
import functools
import math

import jax
import jax.numpy as jnp
from jax import lax
from jax.experimental import pallas as pl
from jax.experimental.pallas import tpu as pltpu
from jax.sharding import PartitionSpec as P

HEADS = 24
HEAD_DIM = 128
TILE = 128
TILES_DEV = 4
REACH = 3
WINDOW = 2 * REACH + 1
ROWS = TILE * TILES_DEV
WIDTH = HEADS * HEAD_DIM
GROUPS = 4
SHARDS = 32
RUNS = 8
EARLY = 2
MIDDLE = RUNS // 2
RING = 4
OWN_HEADS = HEADS // RING
SLOTS = RING + 2 * REACH
KEYS = WINDOW * ROWS
STALE = GROUPS * TILE
BLOCK = 256
HALF = REACH * ROWS // 2
FACTOR = math.log2(math.e) / math.sqrt(HEAD_DIM)
LOW = -1e30
MESH = pl.DeviceIdType.MESH
BF16 = jnp.bfloat16
F32 = jnp.float32


def scores(q, k):
    return lax.dot_general(q, k, (((1,), (1,)), ((), ())), preferred_element_type=F32)


def with_sums(p, v):
    ones = jnp.ones((v.shape[0], HEAD_DIM), BF16)
    return jnp.dot(p, jnp.concatenate([v, ones], axis=1), preferred_element_type=F32)


def kernel(
    q_hbm, k_hbm, v_hbm, sk_hbm, sv_hbm, mask_ref, pick_ref, out_ref,
    kv, qr, ob, oh, stale, stale_out, staging, qh, allow, sc_a, sc_b, top_a, top_b, lse_out, lse_in,
    kv_ss, kv_rs, q_ss, q_rs, halo_ss, halo_rs, relay_rs, pass_ss, o_ss, o_rs, l_ss, l_rs,
    a_ss, a_rs, st_ss, st_rs, loc,
):
    tm = lax.axis_index("tm")
    s = lax.axis_index("seq")
    z = lax.rem(s, RING)
    row0 = s - z
    run = s // RING
    has_low = s >= RING
    has_high = s < SHARDS - RING
    mid_low = run == MIDDLE - 1
    mid_high = run == MIDDLE
    first_run = run == 0
    last_run = run == RUNS - 1
    corner = first_run | mid_low | mid_high | last_run
    near = jnp.where(run < MIDDLE, s + MIDDLE * RING, s - MIDDLE * RING)
    far = jnp.where(first_run | mid_high, s + (MIDDLE - 1) * RING, s - (MIDDLE - 1) * RING)

    def ring(d):
        return (tm, row0 + lax.rem(z + d, RING))

    def group(d):
        return (lax.rem(tm + d, GROUPS), s)

    bar = pltpu.get_barrier_semaphore()
    for d in range(1, RING):
        pl.semaphore_signal(bar, inc=1, device_id=ring(d), device_id_type=MESH)
    for d in range(1, GROUPS):
        pl.semaphore_signal(bar, inc=1, device_id=group(d), device_id_type=MESH)

    @pl.when(has_low)
    def _():
        pl.semaphore_signal(bar, inc=1, device_id=(tm, s - RING), device_id_type=MESH)

    @pl.when(has_high)
    def _():
        pl.semaphore_signal(bar, inc=1, device_id=(tm, s + RING), device_id_type=MESH)

    @pl.when(corner)
    def _():
        pl.semaphore_signal(bar, inc=1, device_id=(tm, near), device_id_type=MESH)
        pl.semaphore_signal(bar, inc=1, device_id=(tm, far), device_id_type=MESH)

    pl.semaphore_wait(
        bar,
        RING - 1 + GROUPS - 1 + has_low.astype(jnp.int32) + has_high.astype(jnp.int32)
        + 2 * corner.astype(jnp.int32),
    )

    def kv_copy(i, d, which):
        src = (k_hbm, v_hbm)[which]
        head = lax.rem(z + d, RING) * OWN_HEADS + i
        cols = pl.ds(pl.multiple_of(head * HEAD_DIM, HEAD_DIM), HEAD_DIM)
        rows = pl.ds(pl.multiple_of((REACH + z) * ROWS, ROWS), ROWS)
        dst = kv.at[i, which, rows, :]
        if d == 0:
            return pltpu.make_async_copy(src.at[:, cols], dst, kv_rs.at[i, d, which])
        return pltpu.make_async_remote_copy(
            src.at[:, cols], dst, kv_ss.at[i, d, which], kv_rs.at[i, d, which],
            device_id=ring(d), device_id_type=MESH)

    def q_copy(i, d):
        head = lax.rem(z + d, RING) * OWN_HEADS + i
        cols = pl.ds(pl.multiple_of(head * HEAD_DIM, HEAD_DIM), HEAD_DIM)
        dst = qr.at[i, pl.ds(pl.multiple_of(z * ROWS, ROWS), ROWS), :]
        if d == 0:
            return pltpu.make_async_copy(q_hbm.at[:, cols], dst, q_rs.at[i, d])
        return pltpu.make_async_remote_copy(
            q_hbm.at[:, cols], dst, q_ss.at[i, d], q_rs.at[i, d],
            device_id=ring(d), device_id_type=MESH)

    def allow_copy(d):
        return pltpu.make_async_remote_copy(
            allow.at[z], allow.at[z], a_ss.at[d], a_rs.at[d],
            device_id=ring(d), device_id_type=MESH)

    LOW_SLOTS, OWN_LOW, OWN_HIGH, HIGH_SLOTS = 0, REACH * ROWS, RING * ROWS, (RING + REACH) * ROWS

    def halo_copy(i, up, half):
        start, land = (OWN_HIGH, LOW_SLOTS) if up else (OWN_LOW, HIGH_SLOTS)
        n = 0 if up else 1
        return pltpu.make_async_remote_copy(
            kv.at[i, :, pl.ds(start + half * HALF, HALF), :],
            kv.at[i, :, pl.ds(land + half * HALF, HALF), :],
            halo_ss.at[i, n, half], halo_rs.at[i, n, half],
            device_id=(tm, s + RING if up else s - RING), device_id_type=MESH)

    def relay_copy(i, up):
        start, land = (OWN_HIGH, HIGH_SLOTS) if up else (OWN_LOW, LOW_SLOTS)
        n = 0 if up else 1
        return pltpu.make_async_remote_copy(
            kv.at[i, :, pl.ds(start + HALF, HALF), :], kv.at[i, :, pl.ds(land, HALF), :],
            halo_ss.at[i, n, 1], relay_rs.at[i], device_id=(tm, near), device_id_type=MESH)

    def pass_copy(i, up):
        start, land = (HIGH_SLOTS, LOW_SLOTS) if up else (LOW_SLOTS, HIGH_SLOTS)
        n = 0 if up else 1
        return pltpu.make_async_remote_copy(
            kv.at[i, :, pl.ds(start, HALF), :], kv.at[i, :, pl.ds(land + HALF, HALF), :],
            pass_ss.at[i], halo_rs.at[i, n, 1], device_id=(tm, far), device_id_type=MESH)

    def hand_on(i):
        @pl.when(last_run)
        def _():
            relay_copy(i, True).wait_recv()
            pass_copy(i, True).start()

        @pl.when(first_run)
        def _():
            relay_copy(i, False).wait_recv()
            pass_copy(i, False).start()

    def o_copy(i, d):
        j = lax.rem(z + d, RING)
        return pltpu.make_async_remote_copy(
            ob.at[i, pl.ds(pl.multiple_of(j * ROWS, ROWS), ROWS), :], oh.at[i, z],
            o_ss.at[i, d], o_rs.at[i, d], device_id=ring(d), device_id_type=MESH)

    def l_copy(i, d):
        j = lax.rem(z + d, RING)
        return pltpu.make_async_remote_copy(
            lse_out.at[i, j], lse_in.at[i, z],
            l_ss.at[i, d], l_rs.at[i, d], device_id=ring(d), device_id_type=MESH)

    def stale_copy(i, d):
        return pltpu.make_async_remote_copy(
            stale_out.at[i, d - 1], stale.at[i, :, pl.ds(pl.multiple_of(tm * TILE, TILE), TILE), :],
            st_ss.at[i, d], st_rs.at[i, d], device_id=group(d), device_id_type=MESH)

    def start_stale(i):
        for d in (2, 1, 3):
            stale_copy(i, d).start()

    def start_kv(i):
        for d in (2, 1, 3, 0):
            for which in range(2):
                kv_copy(i, d, which).start()

    def start_q(i):
        for d in (2, 1, 3, 0):
            q_copy(i, d).start()

    def halo(i):
        for d in range(RING):
            for which in range(2):
                if d == 0:
                    kv_copy(i, d, which).wait()
                else:
                    kv_copy(i, d, which).wait_recv()

        @pl.when(has_high)
        def _():
            halo_copy(i, True, 0).start()

        @pl.when(has_low)
        def _():
            halo_copy(i, False, 0).start()

        @pl.when(has_high & jnp.logical_not(mid_low))
        def _():
            halo_copy(i, True, 1).start()

        @pl.when(has_low & jnp.logical_not(mid_high))
        def _():
            halo_copy(i, False, 1).start()

        @pl.when(mid_low)
        def _():
            relay_copy(i, True).start()

        @pl.when(mid_high)
        def _():
            relay_copy(i, False).start()

    start_kv(0)
    start_q(0)
    pltpu.make_async_copy(q_hbm, qh, loc.at[0]).start()
    pltpu.make_async_copy(sk_hbm, staging.at[0], loc.at[1]).start()
    pltpu.make_async_copy(sv_hbm, staging.at[1], loc.at[2]).start()

    for t in range(TILES_DEV):
        for o in range(WINDOW):
            there = ((s + (o - REACH) >= 0) & (s + (o - REACH) < SHARDS)).astype(F32)
            for j in range(TILES_DEV):
                if o == REACH and j == t:
                    value = jnp.ones((1, TILE), F32)
                else:
                    value = jnp.full((1, TILE), mask_ref[t, j, o], jnp.int32).astype(F32) * there
                allow[z, pl.ds(t * 32 + o * TILES_DEV + j, 1), :] = value
    for d in range(1, RING):
        allow_copy(d).start()

    @pl.loop(1, OWN_HEADS)
    def _(i):
        start_kv(i)
        start_q(i)

    @pl.when(jnp.logical_not(has_low))
    def _():
        @pl.loop(0, OWN_HEADS)
        def _(i):
            for which in range(2):
                kv[i, which, pl.ds(HALF, HALF), :] = jnp.zeros((HALF, HEAD_DIM), BF16)

    @pl.when(jnp.logical_not(has_high))
    def _():
        @pl.loop(0, OWN_HEADS)
        def _(i):
            for which in range(2):
                kv[i, which, pl.ds((RING + REACH) * ROWS + HALF, HALF), :] = jnp.zeros(
                    (HALF, HEAD_DIM), BF16)

    pltpu.make_async_copy(sk_hbm, staging.at[0], loc.at[1]).wait()
    pltpu.make_async_copy(sv_hbm, staging.at[1], loc.at[2]).wait()
    for d in (2, 1, 3, 0):
        tile = pick_ref[0, lax.rem(tm + d, GROUPS)]
        chosen = [
            (1 - jnp.minimum(jnp.abs(jnp.full((TILE, TILE), tile, jnp.int32) - t), 1)).astype(F32).astype(BF16)
            for t in range(TILES_DEV)
        ]
        for which in range(2):
            @pl.loop(0, OWN_HEADS)
            def _(i, d=d, which=which, chosen=chosen):
                for owner in range(RING):
                    cols = pl.ds(pl.multiple_of((owner * OWN_HEADS + i) * HEAD_DIM, HEAD_DIM), HEAD_DIM)
                    one = [staging[which, pl.ds(t * TILE, TILE), cols] * chosen[t] for t in range(TILES_DEV)]
                    one = (one[0] + one[1]) + (one[2] + one[3])
                    place = slice(owner * HEAD_DIM, (owner + 1) * HEAD_DIM)
                    if d == 0:
                        stale[i, which, pl.ds(pl.multiple_of(tm * TILE, TILE), TILE), place] = one
                    else:
                        stale_out[i, d - 1, which, :, place] = one

    halo(0)
    start_stale(0)
    for d in range(1, RING):
        allow_copy(d).wait_recv()
    pltpu.make_async_copy(q_hbm, qh, loc.at[0]).wait()

    def both(i, scored, weighed):
        top = acc = None
        if scored is not None:
            h, b, s_ref, top_ref = scored
            j = lax.rem(z + 1 + h, RING)
            q = qr[i, pl.ds(pl.multiple_of(j * ROWS + b * BLOCK, BLOCK), BLOCK), :]
            base = pl.multiple_of(j * ROWS, ROWS)
        if weighed is not None:
            h2, b2, p_ref, ptop_ref = weighed
            j2 = lax.rem(z + 1 + h2, RING)
            base2 = pl.multiple_of(j2 * ROWS, ROWS)
            shift = ptop_ref[...]
            acc = jnp.zeros((BLOCK, 2 * HEAD_DIM), F32)
        for c in range(WINDOW):
            if scored is not None:
                x = scores(q, kv[i, 0, pl.ds(pl.multiple_of(base + c * ROWS, ROWS), ROWS), :])
                parts = []
                for tt in range(BLOCK // TILE):
                    most = None
                    for kk in range(TILES_DEV):
                        pair = (b * (BLOCK // TILE) + tt) * 32 + c * TILES_DEV + kk
                        y = x[tt * TILE:(tt + 1) * TILE, kk * TILE:(kk + 1) * TILE]
                        y = jnp.where(allow[j, pl.ds(pair, 1), :] > 0, y, LOW)
                        s_ref[tt * TILE:(tt + 1) * TILE, pl.ds(c * ROWS + kk * TILE, TILE)] = y
                        most = y if most is None else jnp.maximum(most, y)
                    parts.append(most)
                x = jnp.concatenate(parts, axis=0)
                top = x if top is None else jnp.maximum(top, x)
            if weighed is not None:
                p = [
                    jnp.exp2(p_ref[:, pl.ds(c * ROWS + kk * TILE, TILE)] * FACTOR - shift).astype(BF16)
                    for kk in range(TILES_DEV)
                ]
                v = kv[i, 1, pl.ds(pl.multiple_of(base2 + c * ROWS, ROWS), ROWS), :]
                acc += with_sums(jnp.concatenate(p, axis=1), v)
        if scored is not None:
            top_ref[...] = jnp.broadcast_to(
                jnp.max(top, axis=1, keepdims=True) * FACTOR, (BLOCK, TILE))
        if weighed is not None:
            total = acc[:, HEAD_DIM:]
            ob[i, pl.ds(pl.multiple_of(j2 * ROWS + b2 * BLOCK, BLOCK), BLOCK), :] = (
                acc[:, :HEAD_DIM] / total).astype(BF16)
            lse = shift + jnp.log2(total)
            for tt in range(BLOCK // TILE):
                turned = lse[tt * TILE:(tt + 1) * TILE, :].T
                lse_out[i, j2, pl.ds(b2 * (BLOCK // TILE) + tt, 1), :] = turned[0:1, :]

    def fresh(i):
        a, b = (sc_a, top_a), (sc_b, top_b)
        both(i, (0, 0, *a), None)

        @pl.loop(0, RING - 1)
        def _(h):
            both(i, (h, 1, *b), (h, 0, *a))
            both(i, (h + 1, 0, *a), (h, 1, *b))
            o_copy(i, h + 1).start()
            l_copy(i, h + 1).start()

        both(i, (RING - 1, 1, *b), (RING - 1, 0, *a))
        both(i, None, (RING - 1, 1, *b))
        oh[i, z] = ob[i, pl.ds(pl.multiple_of(z * ROWS, ROWS), ROWS), :]
        lse_in[i, z] = lse_out[i, z]

    def merge(i):
        for d in range(1, RING):
            o_copy(i, d).wait_recv()
            l_copy(i, d).wait_recv()
            stale_copy(i, d).wait_recv()

        @pl.loop(0, RING * ROWS // BLOCK)
        def _(n):
            owner = n // (ROWS // BLOCK)
            b = n % (ROWS // BLOCK)
            head = owner * OWN_HEADS + i
            cols = pl.ds(pl.multiple_of(head * HEAD_DIM, HEAD_DIM), HEAD_DIM)
            rows = pl.ds(pl.multiple_of(b * BLOCK, BLOCK), BLOCK)
            place = pl.ds(pl.multiple_of(owner * HEAD_DIM, HEAD_DIM), HEAD_DIM)
            x = scores(qh[rows, cols], stale[i, 0, :, place]) * FACTOR
            lse = []
            for tt in range(BLOCK // TILE):
                one = lse_in[i, owner, pl.ds(b * (BLOCK // TILE) + tt, 1), :]
                lse.append(jnp.broadcast_to(one, (TILE, TILE)).T)
            lse = jnp.concatenate(lse, axis=0)
            m = jnp.maximum(jnp.max(x, axis=1, keepdims=True), lse)
            old = jnp.exp2(lse - m)
            p = [jnp.exp2(x[:, k * TILE:(k + 1) * TILE] - m) for k in range(GROUPS)]
            acc = with_sums(jnp.concatenate(p, axis=1).astype(BF16), stale[i, 1, :, place])
            o = oh[i, owner, rows, :].astype(F32)
            out_ref[rows, cols] = (
                (old * o + acc[:, :HEAD_DIM]) / (old + acc[:, HEAD_DIM:])).astype(BF16)

    @pl.loop(0, OWN_HEADS)
    def _(i):
        @pl.when(i < OWN_HEADS - 2)
        def _():
            pass

        @pl.when(i < OWN_HEADS - 1)
        def _():
            halo(i + 1)
            start_stale(i + 1)

        @pl.when(i == 0)
        def _():
            hand_on(0)

        @pl.when(i == OWN_HEADS - 1)
        def _():
            @pl.loop(0, EARLY)
            def _(n):
                merge(n)

        for d in range(RING):
            if d == 0:
                q_copy(i, d).wait()
            else:
                q_copy(i, d).wait_recv()

        @pl.when(has_low)
        def _():
            halo_copy(i, True, 0).wait_recv()
            halo_copy(i, True, 1).wait_recv()

        @pl.when(has_high)
        def _():
            halo_copy(i, False, 0).wait_recv()
            halo_copy(i, False, 1).wait_recv()

        fresh(i)

        @pl.when(i < OWN_HEADS - 1)
        def _():
            hand_on(i + 1)

    @pl.loop(EARLY, OWN_HEADS)
    def _(i):
        merge(i)

    for d in range(1, RING):
        allow_copy(d).wait_send()

    @pl.loop(0, OWN_HEADS)
    def _(i):
        for d in range(1, RING):
            for which in range(2):
                kv_copy(i, d, which).wait_send()
            q_copy(i, d).wait_send()
            o_copy(i, d).wait_send()
            l_copy(i, d).wait_send()
            stale_copy(i, d).wait_send()

        @pl.when(has_high)
        def _():
            halo_copy(i, True, 0).wait_send()
            halo_copy(i, True, 1).wait_send()

        @pl.when(has_low)
        def _():
            halo_copy(i, False, 0).wait_send()
            halo_copy(i, False, 1).wait_send()

        @pl.when(last_run | first_run)
        def _():
            pass_copy(i, True).wait_send()


def body(queries, keys, values, stale_keys, stale_values, tile_mask, stale_pick):
    dma = pltpu.SemaphoreType.DMA
    hbm = pl.BlockSpec(memory_space=pl.ANY)
    smem = pl.BlockSpec(memory_space=pltpu.SMEM)
    return pl.pallas_call(
        kernel,
        out_shape=jax.ShapeDtypeStruct((ROWS, WIDTH), BF16),
        in_specs=[hbm] * 5 + [smem] * 2,
        out_specs=pl.BlockSpec(memory_space=pltpu.VMEM),
        scratch_shapes=[
            pltpu.VMEM((OWN_HEADS, 2, SLOTS * ROWS, HEAD_DIM), BF16),
            pltpu.VMEM((OWN_HEADS, RING * ROWS, HEAD_DIM), BF16),
            pltpu.VMEM((OWN_HEADS, RING * ROWS, HEAD_DIM), BF16),
            pltpu.VMEM((OWN_HEADS, RING, ROWS, HEAD_DIM), BF16),
            pltpu.VMEM((OWN_HEADS, 2, STALE, RING * HEAD_DIM), BF16),
            pltpu.VMEM((OWN_HEADS, GROUPS - 1, 2, TILE, RING * HEAD_DIM), BF16),
            pltpu.VMEM((2, ROWS, WIDTH), BF16),
            pltpu.VMEM((ROWS, WIDTH), BF16),
            pltpu.VMEM((RING, TILE, TILE), F32),
            pltpu.VMEM((BLOCK, KEYS), F32), pltpu.VMEM((BLOCK, KEYS), F32),
            pltpu.VMEM((BLOCK, TILE), F32), pltpu.VMEM((BLOCK, TILE), F32),
            pltpu.VMEM((OWN_HEADS, RING, 8, TILE), F32),
            pltpu.VMEM((OWN_HEADS, RING, 8, TILE), F32),
            dma((OWN_HEADS, RING, 2)), dma((OWN_HEADS, RING, 2)),
            dma((OWN_HEADS, RING)), dma((OWN_HEADS, RING)),
            dma((OWN_HEADS, 2, 2)), dma((OWN_HEADS, 2, 2)),
            dma((OWN_HEADS,)), dma((OWN_HEADS,)),
            dma((OWN_HEADS, RING)), dma((OWN_HEADS, RING)),
            dma((OWN_HEADS, RING)), dma((OWN_HEADS, RING)),
            dma((RING,)), dma((RING,)),
            dma((OWN_HEADS, GROUPS)), dma((OWN_HEADS, GROUPS)),
            dma((3,)),
        ],
        compiler_params=pltpu.CompilerParams(
            collective_id=0, has_side_effects=True, vmem_limit_bytes=58 * 2**20
        ),
        cost_estimate=pl.CostEstimate(
            flops=4 * ROWS * HEAD_DIM * HEADS * (KEYS + STALE),
            bytes_accessed=8 * ROWS * WIDTH * 2,
            transcendentals=ROWS * HEADS * (KEYS + STALE),
        ),
    )(queries, keys, values, stale_keys, stale_values, tile_mask.transpose(0, 2, 1), stale_pick)


def solution(mesh):
    wide = P(("tm", "seq"), None)
    placed = (wide, wide, wide, wide, wide, P(("tm", "seq"), None, None), wide)
    return jax.shard_map(body, mesh=mesh, in_specs=placed, out_specs=wide, check_vma=False)
```

```python
import functools
import math

import jax
import jax.numpy as jnp
from jax import lax
from jax.experimental import pallas as pl
from jax.experimental.pallas import tpu as pltpu
from jax.sharding import PartitionSpec as P

HEADS = 24
HEAD_DIM = 128
TILE = 128
TILES_DEV = 4
REACH = 3
WINDOW = 2 * REACH + 1
ROWS = TILE * TILES_DEV
WIDTH = HEADS * HEAD_DIM
GROUPS = 4
SHARDS = 32
RUNS = 8
EARLY = 2
MIDDLE = RUNS // 2
RING = 4
OWN_HEADS = HEADS // RING
SLOTS = RING + 2 * REACH
KEYS = WINDOW * ROWS
STALE = GROUPS * TILE
BLOCK = 256
HALF = REACH * ROWS // 2
FACTOR = math.log2(math.e) / math.sqrt(HEAD_DIM)
LOW = -1e30
MESH = pl.DeviceIdType.MESH
BF16 = jnp.bfloat16
F32 = jnp.float32


def scores(q, k):
    return lax.dot_general(q, k, (((1,), (1,)), ((), ())), preferred_element_type=F32)


def with_sums(p, v):
    ones = jnp.ones((v.shape[0], HEAD_DIM), BF16)
    return jnp.dot(p, jnp.concatenate([v, ones], axis=1), preferred_element_type=F32)


def kernel(
    q_hbm, k_hbm, v_hbm, sk_hbm, sv_hbm, mask_ref, pick_ref, out_hbm,
    kv, qr, ob, oh, stale, stale_out, staging, qh, allow, sc_a, sc_b, top_a, top_b, lse_out, lse_in, lse_st, merged,
    kv_ss, kv_rs, q_ss, q_rs, halo_ss, halo_rs, relay_rs, pass_ss, o_ss, o_rs, l_ss, l_rs,
    a_ss, a_rs, st_ss, st_rs, loc, out_sem,
):
    tm = lax.axis_index("tm")
    s = lax.axis_index("seq")
    z = lax.rem(s, RING)
    row0 = s - z
    run = s // RING
    has_low = s >= RING
    has_high = s < SHARDS - RING
    mid_low = run == MIDDLE - 1
    mid_high = run == MIDDLE
    first_run = run == 0
    last_run = run == RUNS - 1
    corner = first_run | mid_low | mid_high | last_run
    near = jnp.where(run < MIDDLE, s + MIDDLE * RING, s - MIDDLE * RING)
    far = jnp.where(first_run | mid_high, s + (MIDDLE - 1) * RING, s - (MIDDLE - 1) * RING)

    def ring(d):
        return (tm, row0 + lax.rem(z + d, RING))

    def group(d):
        return (lax.rem(tm + d, GROUPS), s)

    bar = pltpu.get_barrier_semaphore()
    for d in range(1, RING):
        pl.semaphore_signal(bar, inc=1, device_id=ring(d), device_id_type=MESH)
    for d in range(1, GROUPS):
        pl.semaphore_signal(bar, inc=1, device_id=group(d), device_id_type=MESH)

    @pl.when(has_low)
    def _():
        pl.semaphore_signal(bar, inc=1, device_id=(tm, s - RING), device_id_type=MESH)

    @pl.when(has_high)
    def _():
        pl.semaphore_signal(bar, inc=1, device_id=(tm, s + RING), device_id_type=MESH)

    @pl.when(corner)
    def _():
        pl.semaphore_signal(bar, inc=1, device_id=(tm, near), device_id_type=MESH)
        pl.semaphore_signal(bar, inc=1, device_id=(tm, far), device_id_type=MESH)

    pl.semaphore_wait(
        bar,
        RING - 1 + GROUPS - 1 + has_low.astype(jnp.int32) + has_high.astype(jnp.int32)
        + 2 * corner.astype(jnp.int32),
    )

    def kv_copy(i, d, which):
        src = (k_hbm, v_hbm)[which]
        head = lax.rem(z + d, RING) * OWN_HEADS + i
        cols = pl.ds(pl.multiple_of(head * HEAD_DIM, HEAD_DIM), HEAD_DIM)
        rows = pl.ds(pl.multiple_of((REACH + z) * ROWS, ROWS), ROWS)
        dst = kv.at[i, which, rows, :]
        if d == 0:
            return pltpu.make_async_copy(src.at[:, cols], dst, kv_rs.at[i, d, which])
        return pltpu.make_async_remote_copy(
            src.at[:, cols], dst, kv_ss.at[i, d, which], kv_rs.at[i, d, which],
            device_id=ring(d), device_id_type=MESH)

    def q_copy(i, d):
        head = lax.rem(z + d, RING) * OWN_HEADS + i
        cols = pl.ds(pl.multiple_of(head * HEAD_DIM, HEAD_DIM), HEAD_DIM)
        dst = qr.at[i, pl.ds(pl.multiple_of(z * ROWS, ROWS), ROWS), :]
        if d == 0:
            return pltpu.make_async_copy(q_hbm.at[:, cols], dst, q_rs.at[i, d])
        return pltpu.make_async_remote_copy(
            q_hbm.at[:, cols], dst, q_ss.at[i, d], q_rs.at[i, d],
            device_id=ring(d), device_id_type=MESH)

    def allow_copy(d):
        return pltpu.make_async_remote_copy(
            allow.at[z], allow.at[z], a_ss.at[d], a_rs.at[d],
            device_id=ring(d), device_id_type=MESH)

    LOW_SLOTS, OWN_LOW, OWN_HIGH, HIGH_SLOTS = 0, REACH * ROWS, RING * ROWS, (RING + REACH) * ROWS

    def halo_copy(i, up, half, which):
        start, land = (OWN_HIGH, LOW_SLOTS) if up else (OWN_LOW, HIGH_SLOTS)
        n = 0 if up else 1
        return pltpu.make_async_remote_copy(
            kv.at[i, which, pl.ds(start + half * HALF, HALF), :],
            kv.at[i, which, pl.ds(land + half * HALF, HALF), :],
            halo_ss.at[i, n, half, which], halo_rs.at[i, n, half, which],
            device_id=(tm, s + RING if up else s - RING), device_id_type=MESH)

    def relay_copy(i, up, which):
        start, land = (OWN_HIGH, HIGH_SLOTS) if up else (OWN_LOW, LOW_SLOTS)
        n = 0 if up else 1
        return pltpu.make_async_remote_copy(
            kv.at[i, which, pl.ds(start + HALF, HALF), :], kv.at[i, which, pl.ds(land, HALF), :],
            halo_ss.at[i, n, 1, which], relay_rs.at[i, which],
            device_id=(tm, near), device_id_type=MESH)

    def pass_copy(i, up, which):
        start, land = (HIGH_SLOTS, LOW_SLOTS) if up else (LOW_SLOTS, HIGH_SLOTS)
        n = 0 if up else 1
        return pltpu.make_async_remote_copy(
            kv.at[i, which, pl.ds(start, HALF), :], kv.at[i, which, pl.ds(land + HALF, HALF), :],
            pass_ss.at[i, which], halo_rs.at[i, n, 1, which],
            device_id=(tm, far), device_id_type=MESH)

    def hand_on(i):
        for up, here in ((True, last_run), (False, first_run)):
            @pl.when(here)
            def _(up=up):
                for which in range(2):
                    relay_copy(i, up, which).wait_recv()
                    pass_copy(i, up, which).start()

    def o_copy(i, d):
        j = lax.rem(z + d, RING)
        return pltpu.make_async_remote_copy(
            ob.at[i, pl.ds(pl.multiple_of(j * ROWS, ROWS), ROWS), :], oh.at[i, z],
            o_ss.at[i, d], o_rs.at[i, d], device_id=ring(d), device_id_type=MESH)

    def l_copy(i, d):
        j = lax.rem(z + d, RING)
        return pltpu.make_async_remote_copy(
            lse_out.at[i, j], lse_in.at[i, z],
            l_ss.at[i, d], l_rs.at[i, d], device_id=ring(d), device_id_type=MESH)

    def stale_copy(i, d):
        return pltpu.make_async_remote_copy(
            stale_out.at[i, d - 1], stale.at[i, :, pl.ds(pl.multiple_of(tm * TILE, TILE), TILE), :],
            st_ss.at[i, d], st_rs.at[i, d], device_id=group(d), device_id_type=MESH)

    def start_stale(i):
        for d in (2, 1, 3):
            stale_copy(i, d).start()

    def start_kv(i):
        for which in range(2):
            for d in (2, 1, 3, 0):
                kv_copy(i, d, which).start()

    def start_q(i):
        for d in (2, 1, 3, 0):
            q_copy(i, d).start()

    def halo(i):
        for which in range(2):
            for d in range(RING):
                if d == 0:
                    kv_copy(i, d, which).wait()
                else:
                    kv_copy(i, d, which).wait_recv()

            for up, there, mid in ((True, has_high, mid_low), (False, has_low, mid_high)):
                @pl.when(mid)
                def _(up=up, which=which):
                    relay_copy(i, up, which).start()

                @pl.when(there)
                def _(up=up, which=which):
                    halo_copy(i, up, 0, which).start()

                @pl.when(there & jnp.logical_not(mid))
                def _(up=up, which=which):
                    halo_copy(i, up, 1, which).start()

    start_kv(0)
    start_q(0)
    pltpu.make_async_copy(q_hbm, qh, loc.at[0]).start()
    pltpu.make_async_copy(sk_hbm, staging.at[0], loc.at[1]).start()
    pltpu.make_async_copy(sv_hbm, staging.at[1], loc.at[2]).start()

    for t in range(TILES_DEV):
        for o in range(WINDOW):
            there = ((s + (o - REACH) >= 0) & (s + (o - REACH) < SHARDS)).astype(F32)
            for j in range(TILES_DEV):
                if o == REACH and j == t:
                    value = jnp.ones((1, TILE), F32)
                else:
                    value = jnp.full((1, TILE), mask_ref[t, j, o], jnp.int32).astype(F32) * there
                allow[z, pl.ds(t * 32 + o * TILES_DEV + j, 1), :] = value
    for d in range(1, RING):
        allow_copy(d).start()

    @pl.loop(1, OWN_HEADS)
    def _(i):
        start_kv(i)
        start_q(i)

    @pl.when(jnp.logical_not(has_low))
    def _():
        @pl.loop(0, OWN_HEADS)
        def _(i):
            for which in range(2):
                kv[i, which, pl.ds(HALF, HALF), :] = jnp.zeros((HALF, HEAD_DIM), BF16)

    @pl.when(jnp.logical_not(has_high))
    def _():
        @pl.loop(0, OWN_HEADS)
        def _(i):
            for which in range(2):
                kv[i, which, pl.ds((RING + REACH) * ROWS + HALF, HALF), :] = jnp.zeros(
                    (HALF, HEAD_DIM), BF16)

    halo(0)
    pltpu.make_async_copy(sk_hbm, staging.at[0], loc.at[1]).wait()
    pltpu.make_async_copy(sv_hbm, staging.at[1], loc.at[2]).wait()
    for d in (2, 1, 3, 0):
        tile = pick_ref[0, lax.rem(tm + d, GROUPS)]
        chosen = [
            (1 - jnp.minimum(jnp.abs(jnp.full((TILE, TILE), tile, jnp.int32) - t), 1)).astype(F32).astype(BF16)
            for t in range(TILES_DEV)
        ]
        for which in range(2):
            @pl.loop(0, OWN_HEADS)
            def _(i, d=d, which=which, chosen=chosen):
                for owner in range(RING):
                    cols = pl.ds(pl.multiple_of((owner * OWN_HEADS + i) * HEAD_DIM, HEAD_DIM), HEAD_DIM)
                    one = [staging[which, pl.ds(t * TILE, TILE), cols] * chosen[t] for t in range(TILES_DEV)]
                    one = (one[0] + one[1]) + (one[2] + one[3])
                    place = slice(owner * HEAD_DIM, (owner + 1) * HEAD_DIM)
                    if d == 0:
                        stale[i, which, pl.ds(pl.multiple_of(tm * TILE, TILE), TILE), place] = one
                    else:
                        stale_out[i, d - 1, which, :, place] = one

    start_stale(0)
    for d in range(1, RING):
        allow_copy(d).wait_recv()
    pltpu.make_async_copy(q_hbm, qh, loc.at[0]).wait()

    def both(i, scored, weighed):
        top = acc = None
        if scored is not None:
            h, b, s_ref, top_ref = scored
            j = lax.rem(z + 1 + h, RING)
            q = qr[i, pl.ds(pl.multiple_of(j * ROWS + b * BLOCK, BLOCK), BLOCK), :]
            base = pl.multiple_of(j * ROWS, ROWS)
        if weighed is not None:
            h2, b2, p_ref, ptop_ref = weighed
            j2 = lax.rem(z + 1 + h2, RING)
            base2 = pl.multiple_of(j2 * ROWS, ROWS)
            shift = ptop_ref[...]
            acc = jnp.zeros((BLOCK, 2 * HEAD_DIM), F32)
        for c in range(WINDOW):
            if scored is not None:
                x = scores(q, kv[i, 0, pl.ds(pl.multiple_of(base + c * ROWS, ROWS), ROWS), :])
                parts = []
                for tt in range(BLOCK // TILE):
                    most = None
                    for kk in range(TILES_DEV):
                        pair = (b * (BLOCK // TILE) + tt) * 32 + c * TILES_DEV + kk
                        y = x[tt * TILE:(tt + 1) * TILE, kk * TILE:(kk + 1) * TILE]
                        y = jnp.where(allow[j, pl.ds(pair, 1), :] > 0, y, LOW)
                        s_ref[tt * TILE:(tt + 1) * TILE, pl.ds(c * ROWS + kk * TILE, TILE)] = y
                        most = y if most is None else jnp.maximum(most, y)
                    parts.append(most)
                x = jnp.concatenate(parts, axis=0)
                top = x if top is None else jnp.maximum(top, x)
            if weighed is not None:
                p = [
                    jnp.exp2(p_ref[:, pl.ds(c * ROWS + kk * TILE, TILE)] * FACTOR - shift).astype(BF16)
                    for kk in range(TILES_DEV)
                ]
                v = kv[i, 1, pl.ds(pl.multiple_of(base2 + c * ROWS, ROWS), ROWS), :]
                acc += with_sums(jnp.concatenate(p, axis=1), v)
        if scored is not None:
            top_ref[...] = jnp.broadcast_to(
                jnp.max(top, axis=1, keepdims=True) * FACTOR, (BLOCK, TILE))
        if weighed is not None:
            total = acc[:, HEAD_DIM:]
            ob[i, pl.ds(pl.multiple_of(j2 * ROWS + b2 * BLOCK, BLOCK), BLOCK), :] = (
                acc[:, :HEAD_DIM] / total).astype(BF16)
            lse = shift + jnp.log2(total)
            for tt in range(BLOCK // TILE):
                turned = lse[tt * TILE:(tt + 1) * TILE, :].T
                lse_out[i, j2, pl.ds(b2 * (BLOCK // TILE) + tt, 1), :] = turned[0:1, :]

    def fresh(i):
        a, b = (sc_a, top_a), (sc_b, top_b)
        both(i, (0, 0, *a), None)

        @pl.loop(0, RING - 1)
        def _(h):
            both(i, (h, 1, *b), (h, 0, *a))
            both(i, (h + 1, 0, *a), (h, 1, *b))
            o_copy(i, h + 1).start()
            l_copy(i, h + 1).start()

        both(i, (RING - 1, 1, *b), (RING - 1, 0, *a))
        both(i, None, (RING - 1, 1, *b))
        oh[i, z] = ob[i, pl.ds(pl.multiple_of(z * ROWS, ROWS), ROWS), :]
        lse_in[i, z] = lse_out[i, z]

    def columns(owner, i):
        head = owner * OWN_HEADS + i
        return pl.ds(pl.multiple_of(head * HEAD_DIM, HEAD_DIM), HEAD_DIM)

    def apart(i):
        for d in range(1, GROUPS):
            stale_copy(i, d).wait_recv()

        @pl.loop(0, RING * ROWS // BLOCK)
        def _(n):
            owner = n // (ROWS // BLOCK)
            b = n % (ROWS // BLOCK)
            cols = columns(owner, i)
            rows = pl.ds(pl.multiple_of(b * BLOCK, BLOCK), BLOCK)
            place = pl.ds(pl.multiple_of(owner * HEAD_DIM, HEAD_DIM), HEAD_DIM)
            x = scores(qh[rows, cols], stale[i, 0, :, place]) * FACTOR
            m = jnp.max(x, axis=1, keepdims=True)
            acc = with_sums(jnp.exp2(x - m).astype(BF16), stale[i, 1, :, place])
            total = acc[:, HEAD_DIM:]
            merged[rows, cols] = (acc[:, :HEAD_DIM] / total).astype(BF16)
            lse = m + jnp.log2(total)
            for tt in range(BLOCK // TILE):
                turned = lse[tt * TILE:(tt + 1) * TILE, :].T
                lse_st[i, owner, pl.ds(b * (BLOCK // TILE) + tt, 1), :] = turned[0:1, :]

    def out_copy(i, owner):
        cols = columns(owner, i)
        return pltpu.make_async_copy(merged.at[:, cols], out_hbm.at[:, cols], out_sem.at[i, owner])

    def merge(i):
        for d in range(1, RING):
            o_copy(i, d).wait_recv()
            l_copy(i, d).wait_recv()

        @pl.loop(0, RING)
        def _(owner):
            cols = columns(owner, i)
            for t in range(TILES_DEV):
                rows = slice(t * TILE, (t + 1) * TILE)
                share = 1 / (1 + jnp.exp2(lse_st[i, owner, t:t + 1, :] - lse_in[i, owner, t:t + 1, :]))
                share = jnp.broadcast_to(share, (TILE, TILE)).T
                old = merged[rows, cols].astype(F32)
                new = oh[i, owner, rows, :].astype(F32)
                merged[rows, cols] = (old + share * (new - old)).astype(BF16)
            out_copy(i, owner).start()

    @pl.loop(0, OWN_HEADS)
    def _(i):
        @pl.when(i < OWN_HEADS - 1)
        def _():
            halo(i + 1)
            start_stale(i + 1)

        @pl.when(i == 0)
        def _():
            hand_on(0)

        @pl.when(i > 0)
        def _():
            apart(i - 1)

        @pl.when(i == OWN_HEADS - 1)
        def _():
            @pl.loop(0, EARLY)
            def _(n):
                merge(n)

        for d in range(RING):
            if d == 0:
                q_copy(i, d).wait()
            else:
                q_copy(i, d).wait_recv()

        @pl.when(has_low)
        def _():
            for which in range(2):
                halo_copy(i, True, 0, which).wait_recv()
                halo_copy(i, True, 1, which).wait_recv()

        @pl.when(has_high)
        def _():
            for which in range(2):
                halo_copy(i, False, 0, which).wait_recv()
                halo_copy(i, False, 1, which).wait_recv()

        fresh(i)

        @pl.when(i < OWN_HEADS - 1)
        def _():
            hand_on(i + 1)

    apart(OWN_HEADS - 1)

    @pl.loop(EARLY, OWN_HEADS)
    def _(i):
        merge(i)

    for d in range(1, RING):
        allow_copy(d).wait_send()

    @pl.loop(0, OWN_HEADS)
    def _(i):
        out_copy(i, 0).wait()
        for d in range(1, RING):
            for which in range(2):
                kv_copy(i, d, which).wait_send()
            q_copy(i, d).wait_send()
            o_copy(i, d).wait_send()
            l_copy(i, d).wait_send()
            out_copy(i, d).wait()
            stale_copy(i, d).wait_send()

        @pl.when(has_high)
        def _():
            for which in range(2):
                halo_copy(i, True, 0, which).wait_send()
                halo_copy(i, True, 1, which).wait_send()

        @pl.when(has_low)
        def _():
            for which in range(2):
                halo_copy(i, False, 0, which).wait_send()
                halo_copy(i, False, 1, which).wait_send()

        @pl.when(last_run | first_run)
        def _():
            for which in range(2):
                pass_copy(i, True, which).wait_send()


def body(queries, keys, values, stale_keys, stale_values, tile_mask, stale_pick):
    dma = pltpu.SemaphoreType.DMA
    hbm = pl.BlockSpec(memory_space=pl.ANY)
    smem = pl.BlockSpec(memory_space=pltpu.SMEM)
    return pl.pallas_call(
        kernel,
        out_shape=jax.ShapeDtypeStruct((ROWS, WIDTH), BF16),
        in_specs=[hbm] * 5 + [smem] * 2,
        out_specs=hbm,
        scratch_shapes=[
            pltpu.VMEM((OWN_HEADS, 2, SLOTS * ROWS, HEAD_DIM), BF16),
            pltpu.VMEM((OWN_HEADS, RING * ROWS, HEAD_DIM), BF16),
            pltpu.VMEM((OWN_HEADS, RING * ROWS, HEAD_DIM), BF16),
            pltpu.VMEM((OWN_HEADS, RING, ROWS, HEAD_DIM), BF16),
            pltpu.VMEM((OWN_HEADS, 2, STALE, RING * HEAD_DIM), BF16),
            pltpu.VMEM((OWN_HEADS, GROUPS - 1, 2, TILE, RING * HEAD_DIM), BF16),
            pltpu.VMEM((2, ROWS, WIDTH), BF16),
            pltpu.VMEM((ROWS, WIDTH), BF16),
            pltpu.VMEM((RING, TILE, TILE), F32),
            pltpu.VMEM((BLOCK, KEYS), F32), pltpu.VMEM((BLOCK, KEYS), F32),
            pltpu.VMEM((BLOCK, TILE), F32), pltpu.VMEM((BLOCK, TILE), F32),
            pltpu.VMEM((OWN_HEADS, RING, 8, TILE), F32),
            pltpu.VMEM((OWN_HEADS, RING, 8, TILE), F32),
            pltpu.VMEM((OWN_HEADS, RING, 8, TILE), F32),
            pltpu.VMEM((ROWS, WIDTH), BF16),
            dma((OWN_HEADS, RING, 2)), dma((OWN_HEADS, RING, 2)),
            dma((OWN_HEADS, RING)), dma((OWN_HEADS, RING)),
            dma((OWN_HEADS, 2, 2, 2)), dma((OWN_HEADS, 2, 2, 2)),
            dma((OWN_HEADS, 2)), dma((OWN_HEADS, 2)),
            dma((OWN_HEADS, RING)), dma((OWN_HEADS, RING)),
            dma((OWN_HEADS, RING)), dma((OWN_HEADS, RING)),
            dma((RING,)), dma((RING,)),
            dma((OWN_HEADS, GROUPS)), dma((OWN_HEADS, GROUPS)),
            dma((3,)),
            dma((OWN_HEADS, RING)),
        ],
        compiler_params=pltpu.CompilerParams(
            collective_id=0, has_side_effects=True, vmem_limit_bytes=58 * 2**20
        ),
        cost_estimate=pl.CostEstimate(
            flops=4 * ROWS * HEAD_DIM * HEADS * (KEYS + STALE),
            bytes_accessed=8 * ROWS * WIDTH * 2,
            transcendentals=ROWS * HEADS * (KEYS + STALE),
        ),
    )(queries, keys, values, stale_keys, stale_values, tile_mask.transpose(0, 2, 1), stale_pick)


def solution(mesh):
    wide = P(("tm", "seq"), None)
    placed = (wide, wide, wide, wide, wide, P(("tm", "seq"), None, None), wide)
    return jax.shard_map(body, mesh=mesh, in_specs=placed, out_specs=wide, check_vma=False)
```

```python
import functools
import math

import jax
import jax.numpy as jnp
from jax import lax
from jax.experimental import pallas as pl
from jax.experimental.pallas import tpu as pltpu
from jax.sharding import PartitionSpec as P

HEADS = 24
HEAD_DIM = 128
TILE = 128
TILES_DEV = 4
REACH = 3
WINDOW = 2 * REACH + 1
ROWS = TILE * TILES_DEV
WIDTH = HEADS * HEAD_DIM
GROUPS = 4
SHARDS = 32
RUNS = 8
EARLY = 2
MIDDLE = RUNS // 2
RING = 4
OWN_HEADS = HEADS // RING
SLOTS = RING + 2 * REACH
KEYS = WINDOW * ROWS
STALE = GROUPS * TILE
BLOCK = 256
HALF = REACH * ROWS // 2
FACTOR = math.log2(math.e) / math.sqrt(HEAD_DIM)
LOW = -1e30
MESH = pl.DeviceIdType.MESH
BF16 = jnp.bfloat16
F32 = jnp.float32


def scores(q, k):
    return lax.dot_general(q, k, (((1,), (1,)), ((), ())), preferred_element_type=F32)


def with_sums(p, v):
    ones = jnp.ones((v.shape[0], HEAD_DIM), BF16)
    return jnp.dot(p, jnp.concatenate([v, ones], axis=1), preferred_element_type=F32)


def kernel(
    q_hbm, k_hbm, v_hbm, sk_hbm, sv_hbm, mask_ref, pick_ref, out_hbm,
    kv, qr, ob, oh, stale, stale_out, staging, qh, allow, sc_a, sc_b, top_a, top_b, lse_out, lse_in, lse_st, merged, packed,
    kv_ss, kv_rs, q_ss, q_rs, halo_ss, halo_rs, relay_rs, pass_ss, o_ss, o_rs, l_ss, l_rs,
    a_ss, a_rs, st_ss, st_rs, loc, out_sem,
):
    tm = lax.axis_index("tm")
    s = lax.axis_index("seq")
    z = lax.rem(s, RING)
    row0 = s - z
    run = s // RING
    has_low = s >= RING
    has_high = s < SHARDS - RING
    mid_low = run == MIDDLE - 1
    mid_high = run == MIDDLE
    first_run = run == 0
    last_run = run == RUNS - 1
    corner = first_run | mid_low | mid_high | last_run
    near = jnp.where(run < MIDDLE, s + MIDDLE * RING, s - MIDDLE * RING)
    far = jnp.where(first_run | mid_high, s + (MIDDLE - 1) * RING, s - (MIDDLE - 1) * RING)

    def ring(d):
        return (tm, row0 + lax.rem(z + d, RING))

    def group(d):
        return (lax.rem(tm + d, GROUPS), s)

    bar = pltpu.get_barrier_semaphore()
    for d in range(1, RING):
        pl.semaphore_signal(bar, inc=1, device_id=ring(d), device_id_type=MESH)
    for d in range(1, GROUPS):
        pl.semaphore_signal(bar, inc=1, device_id=group(d), device_id_type=MESH)

    @pl.when(has_low)
    def _():
        pl.semaphore_signal(bar, inc=1, device_id=(tm, s - RING), device_id_type=MESH)

    @pl.when(has_high)
    def _():
        pl.semaphore_signal(bar, inc=1, device_id=(tm, s + RING), device_id_type=MESH)

    @pl.when(corner)
    def _():
        pl.semaphore_signal(bar, inc=1, device_id=(tm, near), device_id_type=MESH)
        pl.semaphore_signal(bar, inc=1, device_id=(tm, far), device_id_type=MESH)

    pl.semaphore_wait(
        bar,
        RING - 1 + GROUPS - 1 + has_low.astype(jnp.int32) + has_high.astype(jnp.int32)
        + 2 * corner.astype(jnp.int32),
    )

    def kv_copy(i, d, which):
        src = (k_hbm, v_hbm)[which]
        head = lax.rem(z + d, RING) * OWN_HEADS + i
        cols = pl.ds(pl.multiple_of(head * HEAD_DIM, HEAD_DIM), HEAD_DIM)
        rows = pl.ds(pl.multiple_of((REACH + z) * ROWS, ROWS), ROWS)
        dst = kv.at[i, which, rows, :]
        if d == 0:
            return pltpu.make_async_copy(src.at[:, cols], dst, kv_rs.at[i, d, which])
        return pltpu.make_async_remote_copy(
            src.at[:, cols], dst, kv_ss.at[i, d, which], kv_rs.at[i, d, which],
            device_id=ring(d), device_id_type=MESH)

    def q_copy(i, d):
        head = lax.rem(z + d, RING) * OWN_HEADS + i
        cols = pl.ds(pl.multiple_of(head * HEAD_DIM, HEAD_DIM), HEAD_DIM)
        dst = qr.at[i, pl.ds(pl.multiple_of(z * ROWS, ROWS), ROWS), :]
        if d == 0:
            return pltpu.make_async_copy(q_hbm.at[:, cols], dst, q_rs.at[i, d])
        return pltpu.make_async_remote_copy(
            q_hbm.at[:, cols], dst, q_ss.at[i, d], q_rs.at[i, d],
            device_id=ring(d), device_id_type=MESH)

    def allow_copy(d):
        return pltpu.make_async_remote_copy(
            packed.at[z], packed.at[z], a_ss.at[d], a_rs.at[d],
            device_id=ring(d), device_id_type=MESH)

    LOW_SLOTS, OWN_LOW, OWN_HIGH, HIGH_SLOTS = 0, REACH * ROWS, RING * ROWS, (RING + REACH) * ROWS

    def halo_copy(i, up, half, which):
        start, land = (OWN_HIGH, LOW_SLOTS) if up else (OWN_LOW, HIGH_SLOTS)
        n = 0 if up else 1
        return pltpu.make_async_remote_copy(
            kv.at[i, which, pl.ds(start + half * HALF, HALF), :],
            kv.at[i, which, pl.ds(land + half * HALF, HALF), :],
            halo_ss.at[i, n, half, which], halo_rs.at[i, n, half, which],
            device_id=(tm, s + RING if up else s - RING), device_id_type=MESH)

    def relay_copy(i, up, which):
        start, land = (OWN_HIGH, HIGH_SLOTS) if up else (OWN_LOW, LOW_SLOTS)
        n = 0 if up else 1
        return pltpu.make_async_remote_copy(
            kv.at[i, which, pl.ds(start + HALF, HALF), :], kv.at[i, which, pl.ds(land, HALF), :],
            halo_ss.at[i, n, 1, which], relay_rs.at[i, which],
            device_id=(tm, near), device_id_type=MESH)

    def pass_copy(i, up, which):
        start, land = (HIGH_SLOTS, LOW_SLOTS) if up else (LOW_SLOTS, HIGH_SLOTS)
        n = 0 if up else 1
        return pltpu.make_async_remote_copy(
            kv.at[i, which, pl.ds(start, HALF), :], kv.at[i, which, pl.ds(land + HALF, HALF), :],
            pass_ss.at[i, which], halo_rs.at[i, n, 1, which],
            device_id=(tm, far), device_id_type=MESH)

    def hand_on(i):
        for up, here in ((True, last_run), (False, first_run)):
            @pl.when(here)
            def _(up=up):
                for which in range(2):
                    relay_copy(i, up, which).wait_recv()
                    pass_copy(i, up, which).start()

    def o_copy(i, d):
        j = lax.rem(z + d, RING)
        return pltpu.make_async_remote_copy(
            ob.at[i, pl.ds(pl.multiple_of(j * ROWS, ROWS), ROWS), :], oh.at[i, z],
            o_ss.at[i, d], o_rs.at[i, d], device_id=ring(d), device_id_type=MESH)

    def l_copy(i, d):
        j = lax.rem(z + d, RING)
        return pltpu.make_async_remote_copy(
            lse_out.at[i, j], lse_in.at[i, z],
            l_ss.at[i, d], l_rs.at[i, d], device_id=ring(d), device_id_type=MESH)

    def stale_copy(i, d):
        return pltpu.make_async_remote_copy(
            stale_out.at[i, d - 1], stale.at[i, :, pl.ds(pl.multiple_of(tm * TILE, TILE), TILE), :],
            st_ss.at[i, d], st_rs.at[i, d], device_id=group(d), device_id_type=MESH)

    def start_stale(i):
        for d in (2, 1, 3):
            stale_copy(i, d).start()

    def start_kv(i):
        for which in range(2):
            for d in (2, 1, 3, 0):
                kv_copy(i, d, which).start()

    def start_q(i):
        for d in (2, 1, 3, 0):
            q_copy(i, d).start()

    def halo(i, which):
        for d in range(RING):
            if d == 0:
                kv_copy(i, d, which).wait()
            else:
                kv_copy(i, d, which).wait_recv()

        for up, there, mid in ((True, has_high, mid_low), (False, has_low, mid_high)):
            @pl.when(mid)
            def _(up=up):
                relay_copy(i, up, which).start()

            @pl.when(there)
            def _(up=up):
                halo_copy(i, up, 0, which).start()

            @pl.when(there & jnp.logical_not(mid))
            def _(up=up):
                halo_copy(i, up, 1, which).start()

    start_kv(0)
    start_q(0)
    pltpu.make_async_copy(sk_hbm, staging.at[0], loc.at[1]).start()
    pltpu.make_async_copy(sv_hbm, staging.at[1], loc.at[2]).start()
    pltpu.make_async_copy(q_hbm, qh, loc.at[0]).start()

    for t in range(TILES_DEV):
        for o in range(WINDOW):
            there = ((s + (o - REACH) >= 0) & (s + (o - REACH) < SHARDS)).astype(F32)
            for j in range(TILES_DEV):
                if o == REACH and j == t:
                    value = jnp.ones((1, TILE), F32)
                else:
                    value = jnp.full((1, TILE), mask_ref[t, j, o], jnp.int32).astype(F32) * there
                allow[z, pl.ds(t * 32 + o * TILES_DEV + j, 1), :] = value
    for t in range(TILES_DEV):
        allow[z, pl.ds(t * 32 + 28, 4), :] = jnp.zeros((4, TILE), F32)
    packed[z] = allow[z].T[0:8, :]
    for d in range(1, RING):
        allow_copy(d).start()

    @pl.loop(1, OWN_HEADS)
    def _(i):
        start_kv(i)
        start_q(i)

    @pl.when(jnp.logical_not(has_low))
    def _():
        @pl.loop(0, OWN_HEADS)
        def _(i):
            for which in range(2):
                kv[i, which, pl.ds(HALF, HALF), :] = jnp.zeros((HALF, HEAD_DIM), BF16)

    @pl.when(jnp.logical_not(has_high))
    def _():
        @pl.loop(0, OWN_HEADS)
        def _(i):
            for which in range(2):
                kv[i, which, pl.ds((RING + REACH) * ROWS + HALF, HALF), :] = jnp.zeros(
                    (HALF, HEAD_DIM), BF16)

    halo(0, 0)
    pltpu.make_async_copy(sk_hbm, staging.at[0], loc.at[1]).wait()
    pltpu.make_async_copy(sv_hbm, staging.at[1], loc.at[2]).wait()
    for d in (2, 1, 3, 0):
        tile = pick_ref[0, lax.rem(tm + d, GROUPS)]
        chosen = [
            (1 - jnp.minimum(jnp.abs(jnp.full((TILE, TILE), tile, jnp.int32) - t), 1)).astype(F32).astype(BF16)
            for t in range(TILES_DEV)
        ]
        for which in range(2):
            @pl.loop(0, OWN_HEADS)
            def _(i, d=d, which=which, chosen=chosen):
                for owner in range(RING):
                    cols = pl.ds(pl.multiple_of((owner * OWN_HEADS + i) * HEAD_DIM, HEAD_DIM), HEAD_DIM)
                    one = [staging[which, pl.ds(t * TILE, TILE), cols] * chosen[t] for t in range(TILES_DEV)]
                    one = (one[0] + one[1]) + (one[2] + one[3])
                    place = slice(owner * HEAD_DIM, (owner + 1) * HEAD_DIM)
                    if d == 0:
                        stale[i, which, pl.ds(pl.multiple_of(tm * TILE, TILE), TILE), place] = one
                    else:
                        stale_out[i, d - 1, which, :, place] = one

    start_stale(0)
    halo(0, 1)
    for d in range(1, RING):
        allow_copy(d).wait_recv()
        j = lax.rem(z + RING - d, RING)
        allow[j] = jnp.broadcast_to(packed[j, 0:1, :], (TILE, TILE)).T
    pltpu.make_async_copy(q_hbm, qh, loc.at[0]).wait()

    def both(i, scored, weighed):
        top = acc = None
        if scored is not None:
            h, b, s_ref, top_ref = scored
            j = lax.rem(z + 1 + h, RING)
            q = qr[i, pl.ds(pl.multiple_of(j * ROWS + b * BLOCK, BLOCK), BLOCK), :]
            base = pl.multiple_of(j * ROWS, ROWS)
        if weighed is not None:
            h2, b2, p_ref, ptop_ref = weighed
            j2 = lax.rem(z + 1 + h2, RING)
            base2 = pl.multiple_of(j2 * ROWS, ROWS)
            shift = ptop_ref[...]
            acc = jnp.zeros((BLOCK, 2 * HEAD_DIM), F32)
        for c in range(WINDOW):
            if scored is not None:
                x = scores(q, kv[i, 0, pl.ds(pl.multiple_of(base + c * ROWS, ROWS), ROWS), :])
                parts = []
                for tt in range(BLOCK // TILE):
                    most = None
                    for kk in range(TILES_DEV):
                        pair = (b * (BLOCK // TILE) + tt) * 32 + c * TILES_DEV + kk
                        y = x[tt * TILE:(tt + 1) * TILE, kk * TILE:(kk + 1) * TILE]
                        y = jnp.where(allow[j, pl.ds(pair, 1), :] > 0, y, LOW)
                        s_ref[tt * TILE:(tt + 1) * TILE, pl.ds(c * ROWS + kk * TILE, TILE)] = y
                        most = y if most is None else jnp.maximum(most, y)
                    parts.append(most)
                x = jnp.concatenate(parts, axis=0)
                top = x if top is None else jnp.maximum(top, x)
            if weighed is not None:
                p = [
                    jnp.exp2(p_ref[:, pl.ds(c * ROWS + kk * TILE, TILE)] * FACTOR - shift).astype(BF16)
                    for kk in range(TILES_DEV)
                ]
                v = kv[i, 1, pl.ds(pl.multiple_of(base2 + c * ROWS, ROWS), ROWS), :]
                acc += with_sums(jnp.concatenate(p, axis=1), v)
        if scored is not None:
            top_ref[...] = jnp.broadcast_to(
                jnp.max(top, axis=1, keepdims=True) * FACTOR, (BLOCK, TILE))
        if weighed is not None:
            total = acc[:, HEAD_DIM:]
            ob[i, pl.ds(pl.multiple_of(j2 * ROWS + b2 * BLOCK, BLOCK), BLOCK), :] = (
                acc[:, :HEAD_DIM] / total).astype(BF16)
            lse = shift + jnp.log2(total)
            for tt in range(BLOCK // TILE):
                turned = lse[tt * TILE:(tt + 1) * TILE, :].T
                lse_out[i, j2, pl.ds(b2 * (BLOCK // TILE) + tt, 1), :] = turned[0:1, :]

    def fresh(i):
        a, b = (sc_a, top_a), (sc_b, top_b)
        both(i, (0, 0, *a), None)

        @pl.loop(0, RING - 1)
        def _(h):
            both(i, (h, 1, *b), (h, 0, *a))
            both(i, (h + 1, 0, *a), (h, 1, *b))
            o_copy(i, h + 1).start()
            l_copy(i, h + 1).start()

        both(i, (RING - 1, 1, *b), (RING - 1, 0, *a))
        both(i, None, (RING - 1, 1, *b))
        oh[i, z] = ob[i, pl.ds(pl.multiple_of(z * ROWS, ROWS), ROWS), :]
        lse_in[i, z] = lse_out[i, z]

    def columns(owner, i):
        head = owner * OWN_HEADS + i
        return pl.ds(pl.multiple_of(head * HEAD_DIM, HEAD_DIM), HEAD_DIM)

    def apart(i):
        for d in range(1, GROUPS):
            stale_copy(i, d).wait_recv()

        @pl.loop(0, RING * ROWS // BLOCK)
        def _(n):
            owner = n // (ROWS // BLOCK)
            b = n % (ROWS // BLOCK)
            cols = columns(owner, i)
            rows = pl.ds(pl.multiple_of(b * BLOCK, BLOCK), BLOCK)
            place = pl.ds(pl.multiple_of(owner * HEAD_DIM, HEAD_DIM), HEAD_DIM)
            x = scores(qh[rows, cols], stale[i, 0, :, place]) * FACTOR
            m = jnp.max(x, axis=1, keepdims=True)
            acc = with_sums(jnp.exp2(x - m).astype(BF16), stale[i, 1, :, place])
            total = acc[:, HEAD_DIM:]
            merged[rows, cols] = (acc[:, :HEAD_DIM] / total).astype(BF16)
            lse = m + jnp.log2(total)
            for tt in range(BLOCK // TILE):
                turned = lse[tt * TILE:(tt + 1) * TILE, :].T
                lse_st[i, owner, pl.ds(b * (BLOCK // TILE) + tt, 1), :] = turned[0:1, :]

    def out_copy(i, owner):
        cols = columns(owner, i)
        return pltpu.make_async_copy(merged.at[:, cols], out_hbm.at[:, cols], out_sem.at[i, owner])

    def merge(i):
        for d in range(1, RING):
            o_copy(i, d).wait_recv()
            l_copy(i, d).wait_recv()

        @pl.loop(0, RING)
        def _(owner):
            cols = columns(owner, i)
            for t in range(TILES_DEV):
                rows = slice(t * TILE, (t + 1) * TILE)
                share = 1 / (1 + jnp.exp2(lse_st[i, owner, t:t + 1, :] - lse_in[i, owner, t:t + 1, :]))
                share = jnp.broadcast_to(share, (TILE, TILE)).T
                old = merged[rows, cols].astype(F32)
                new = oh[i, owner, rows, :].astype(F32)
                merged[rows, cols] = (old + share * (new - old)).astype(BF16)
            out_copy(i, owner).start()

    @pl.loop(0, OWN_HEADS)
    def _(i):
        @pl.when(i < OWN_HEADS - 1)
        def _():
            halo(i + 1, 0)
            halo(i + 1, 1)
            start_stale(i + 1)

        @pl.when(i == 0)
        def _():
            hand_on(0)

        @pl.when(i > 0)
        def _():
            apart(i - 1)

        @pl.when(i == OWN_HEADS - 1)
        def _():
            @pl.loop(0, EARLY)
            def _(n):
                merge(n)

        for d in range(RING):
            if d == 0:
                q_copy(i, d).wait()
            else:
                q_copy(i, d).wait_recv()

        @pl.when(has_low)
        def _():
            for which in range(2):
                halo_copy(i, True, 0, which).wait_recv()
                halo_copy(i, True, 1, which).wait_recv()

        @pl.when(has_high)
        def _():
            for which in range(2):
                halo_copy(i, False, 0, which).wait_recv()
                halo_copy(i, False, 1, which).wait_recv()

        fresh(i)

        @pl.when(i < OWN_HEADS - 1)
        def _():
            hand_on(i + 1)

    @pl.loop(EARLY, OWN_HEADS)
    def _(i):
        @pl.when(i == OWN_HEADS - 1)
        def _():
            apart(i)

        merge(i)

    for d in range(1, RING):
        allow_copy(d).wait_send()

    @pl.loop(0, OWN_HEADS)
    def _(i):
        out_copy(i, 0).wait()
        for d in range(1, RING):
            for which in range(2):
                kv_copy(i, d, which).wait_send()
            q_copy(i, d).wait_send()
            o_copy(i, d).wait_send()
            l_copy(i, d).wait_send()
            out_copy(i, d).wait()
            stale_copy(i, d).wait_send()

        @pl.when(has_high)
        def _():
            for which in range(2):
                halo_copy(i, True, 0, which).wait_send()
                halo_copy(i, True, 1, which).wait_send()

        @pl.when(has_low)
        def _():
            for which in range(2):
                halo_copy(i, False, 0, which).wait_send()
                halo_copy(i, False, 1, which).wait_send()

        @pl.when(last_run | first_run)
        def _():
            for which in range(2):
                pass_copy(i, True, which).wait_send()


def body(queries, keys, values, stale_keys, stale_values, tile_mask, stale_pick):
    dma = pltpu.SemaphoreType.DMA
    hbm = pl.BlockSpec(memory_space=pl.ANY)
    smem = pl.BlockSpec(memory_space=pltpu.SMEM)
    return pl.pallas_call(
        kernel,
        out_shape=jax.ShapeDtypeStruct((ROWS, WIDTH), BF16),
        in_specs=[hbm] * 5 + [smem] * 2,
        out_specs=hbm,
        scratch_shapes=[
            pltpu.VMEM((OWN_HEADS, 2, SLOTS * ROWS, HEAD_DIM), BF16),
            pltpu.VMEM((OWN_HEADS, RING * ROWS, HEAD_DIM), BF16),
            pltpu.VMEM((OWN_HEADS, RING * ROWS, HEAD_DIM), BF16),
            pltpu.VMEM((OWN_HEADS, RING, ROWS, HEAD_DIM), BF16),
            pltpu.VMEM((OWN_HEADS, 2, STALE, RING * HEAD_DIM), BF16),
            pltpu.VMEM((OWN_HEADS, GROUPS - 1, 2, TILE, RING * HEAD_DIM), BF16),
            pltpu.VMEM((2, ROWS, WIDTH), BF16),
            pltpu.VMEM((ROWS, WIDTH), BF16),
            pltpu.VMEM((RING, TILE, TILE), F32),
            pltpu.VMEM((BLOCK, KEYS), F32), pltpu.VMEM((BLOCK, KEYS), F32),
            pltpu.VMEM((BLOCK, TILE), F32), pltpu.VMEM((BLOCK, TILE), F32),
            pltpu.VMEM((OWN_HEADS, RING, 8, TILE), F32),
            pltpu.VMEM((OWN_HEADS, RING, 8, TILE), F32),
            pltpu.VMEM((OWN_HEADS, RING, 8, TILE), F32),
            pltpu.VMEM((ROWS, WIDTH), BF16),
            pltpu.VMEM((RING, 8, TILE), F32),
            dma((OWN_HEADS, RING, 2)), dma((OWN_HEADS, RING, 2)),
            dma((OWN_HEADS, RING)), dma((OWN_HEADS, RING)),
            dma((OWN_HEADS, 2, 2, 2)), dma((OWN_HEADS, 2, 2, 2)),
            dma((OWN_HEADS, 2)), dma((OWN_HEADS, 2)),
            dma((OWN_HEADS, RING)), dma((OWN_HEADS, RING)),
            dma((OWN_HEADS, RING)), dma((OWN_HEADS, RING)),
            dma((RING,)), dma((RING,)),
            dma((OWN_HEADS, GROUPS)), dma((OWN_HEADS, GROUPS)),
            dma((3,)),
            dma((OWN_HEADS, RING)),
        ],
        compiler_params=pltpu.CompilerParams(
            collective_id=0, has_side_effects=True, vmem_limit_bytes=58 * 2**20
        ),
        cost_estimate=pl.CostEstimate(
            flops=4 * ROWS * HEAD_DIM * HEADS * (KEYS + STALE),
            bytes_accessed=8 * ROWS * WIDTH * 2,
            transcendentals=ROWS * HEADS * (KEYS + STALE),
        ),
    )(queries, keys, values, stale_keys, stale_values, tile_mask.transpose(0, 2, 1), stale_pick)


def solution(mesh):
    wide = P(("tm", "seq"), None)
    placed = (wide, wide, wide, wide, wide, P(("tm", "seq"), None, None), wide)
    return jax.shard_map(body, mesh=mesh, in_specs=placed, out_specs=wide, check_vma=False)
```
